128 devices in a mesh: seq: 16 (over x, y), pipe: 8 (over z, core).
Axes of the slice: x: 4, y: 4, z: 4, core: 2. Of those that a mesh axis runs over, the one named last changes fastest.
Arguments:
- query_in: bfloat16 [8, 2048, 4096], P('pipe', 'seq'), may hold values from -6 to 6
- key_in: bfloat16 [8, 2048, 4096], P('pipe', 'seq'), may hold values from -6 to 6
- value_in: bfloat16 [8, 2048, 4096], P('pipe', 'seq'), may hold values from -6 to 6
- grad_out: bfloat16 [8, 2048, 4096], P('pipe', 'seq'), may hold values from -6 to 6
- long_filter: float32 [8, 2048, 256], P('pipe', 'seq'), may hold values from -2 to 2, as said below
- short_taps: float32 [8, 3, 3, 4096], P('pipe'), may hold values from -3 to 3
Outputs:
- layer_out: bfloat16 [8, 2048, 4096], P('pipe', 'seq')
- passed_grads: bfloat16 [8, 3, 2048, 4096], P('pipe', None, 'seq')
- filter_grad: float32 [8, 2048, 256], P('pipe', 'seq')
- tap_grads: float32 [8, 3, 3, 4096], P('pipe')
The draws below stay inside these ranges and needn't reach their ends.
Inputs may be any that keep to these rules, and one draw needn't show every extreme that they name: `long_filter`: one filter for each channel group of each section.
All inputs are finite; a program needn't handle non-finite values.
Results may differ from the reference program's by a relative error of at most 0.005.
Values may be sent and summed in bfloat16 or wider, within the bound.
A program may use at most 256 MiB of HBM per device.

```python
import math
import jax
import jax.numpy as jnp
from jax import lax

GW = 16
GROUP_COUNT = 256
D = 4096
TAPS = 3
TOKEN_LENGTH = 2048
SECTION_COUNT = 8


def draw_long_filter(key, part):
    split_random_keys = jax.random.split(key, 7)
    slow_count = 5
    random_noise = jnp.clip(jax.random.normal(split_random_keys[0], (SECTION_COUNT, TOKEN_LENGTH, GROUP_COUNT)), -4.0, 4.0)
    is_slow = jax.random.randint(split_random_keys[1], (SECTION_COUNT, 1, GROUP_COUNT), 0, 10) < slow_count
    slow_rate = jnp.exp(jax.random.uniform(split_random_keys[2], (SECTION_COUNT, 1, GROUP_COUNT), minval=math.log(0.25), maxval=math.log(0.5))) / TOKEN_LENGTH
    fast_rate = jnp.exp(jax.random.uniform(split_random_keys[3], (SECTION_COUNT, 1, GROUP_COUNT), minval=math.log(0.02), maxval=math.log(0.05)))
    spike_position = jax.random.randint(split_random_keys[4], (SECTION_COUNT, 1, GROUP_COUNT, 2), 1, TOKEN_LENGTH)
    spike_height = jax.random.uniform(split_random_keys[5], (SECTION_COUNT, 1, GROUP_COUNT, 2), minval=0.22, maxval=0.69)
    tail_share = jax.random.uniform(split_random_keys[6], (SECTION_COUNT, 1, GROUP_COUNT), minval=0.2, maxval=0.3)
    token_place = jnp.arange(TOKEN_LENGTH, dtype=jnp.int32)
    reached_mask = (token_place[None, :, None, None] >= spike_position).astype(jnp.float32)
    spike_total = jnp.sum(reached_mask * spike_height, axis=3)
    step_values_real = token_place.astype(jnp.float32)[None, :, None]
    slow_amplitude = jnp.sqrt(1.0 - jnp.exp(-2.0 * slow_rate))
    fast_amplitude = jnp.sqrt(1.0 - jnp.exp(-2.0 * fast_rate))
    lasting = jnp.exp(-slow_rate * step_values_real - spike_total)
    fading = jnp.exp(-fast_rate * step_values_real)
    envelope = jnp.where(is_slow, slow_amplitude * lasting, fast_amplitude * (fading + tail_share * lasting))
    return random_noise * envelope


def levels(own_key, dims, shards, least, largest):
    factor_of = 1.0
    for dim, blocks in shards:
        draws = jax.random.uniform(jax.random.fold_in(jax.random.fold_in(own_key, 6), dim), (blocks,), jnp.float32, least / len(shards), largest / len(shards))
        factor_of = factor_of * jnp.repeat(jnp.exp(draws), dims[dim] // blocks).reshape((-1,) + (1,) * (len(dims) - 1 - dim))
    return factor_of


def bell_draw(key, dims, spread, limit, pieces=(), kind=jnp.bfloat16):
    loudness = levels(key, dims, pieces, -0.22, 0.18) if pieces else 1.0
    drawn = jax.random.normal(key, dims, jnp.float32) * spread * loudness
    return jnp.minimum(jnp.maximum(drawn, -limit), limit).astype(kind)


def setup_inputs(seed: int = 0) -> dict:
    arg_keys = jax.random.split(jax.random.key(seed), 7)
    return {
        "query_in": bell_draw(arg_keys[0], (SECTION_COUNT, TOKEN_LENGTH, D), 1.0, 6.0, ((0, 8), (1, 16))),
        "key_in": bell_draw(arg_keys[1], (SECTION_COUNT, TOKEN_LENGTH, D), 1.0, 6.0, ((0, 8), (1, 16))),
        "value_in": bell_draw(arg_keys[2], (SECTION_COUNT, TOKEN_LENGTH, D), 1.0, 6.0, ((0, 8), (1, 16))),
        "grad_out": bell_draw(arg_keys[3], (SECTION_COUNT, TOKEN_LENGTH, D), 1.0, 6.0, ((0, 8), (1, 16))),
        "long_filter": draw_long_filter(jax.random.fold_in(arg_keys[6], 71), 0),
        "short_taps": bell_draw(arg_keys[5], (SECTION_COUNT, 3, TAPS, D), 0.6, 3.0, ((0, 8),), jnp.float32),
    }


def short_filter(tap_table, padded, length):
    result = tap_table[:, 0, None, :] * padded[:, 2:2 + length, :]
    result = result + tap_table[:, 1, None, :] * padded[:, 1:1 + length, :]
    result = result + tap_table[:, 2, None, :] * padded[:, 0:length, :]
    return result

def one_section(inputs):
    query_in, key_in, value_in, grad_out, long_filter, short_taps = inputs
    length = query_in.shape[0]
    fft_size = 2 * length
    stacked_in = jnp.stack([query_in, key_in, value_in]).astype(jnp.float32)
    padded = jnp.pad(stacked_in, ((0, 0), (2, 0), (0, 0)))
    featured = short_filter(short_taps, padded, length)
    query_feat = featured[0]
    keyed = featured[1]
    valued = featured[2]
    grad_float = grad_out.astype(jnp.float32)
    product = (keyed * valued).astype(jnp.bfloat16)
    scaled = (grad_float * query_feat).astype(jnp.bfloat16)
    filter_spec = jnp.fft.rfft(long_filter, n=fft_size, axis=0)
    kernel = jnp.repeat(filter_spec, GW, axis=1)
    prod_spec = jnp.fft.rfft(product.astype(jnp.float32), n=fft_size, axis=0)
    conv_out = jnp.fft.irfft(prod_spec * kernel, n=fft_size, axis=0)[:length]
    layer_out = (query_feat * conv_out).astype(jnp.bfloat16)
    scaled_spec = jnp.fft.rfft(scaled.astype(jnp.float32), n=fft_size, axis=0)
    back_out = jnp.fft.irfft(scaled_spec * jnp.conj(kernel), n=fft_size, axis=0)[:length]
    cross_spec = (scaled_spec * jnp.conj(prod_spec)).reshape(-1, GROUP_COUNT, GW).sum(axis=2)
    filter_grad = jnp.fft.irfft(cross_spec, n=fft_size, axis=0)[:length] / math.sqrt(length * GW)
    grad_stack = jnp.stack([grad_float * conv_out, back_out * valued, back_out * keyed])
    after_rows = jnp.pad(grad_stack, ((0, 0), (0, 2), (0, 0)))
    input_grads = short_taps[:, 0, None, :] * after_rows[:, 0:length, :]
    input_grads = input_grads + short_taps[:, 1, None, :] * after_rows[:, 1:1 + length, :]
    input_grads = input_grads + short_taps[:, 2, None, :] * after_rows[:, 2:2 + length, :]
    input_grads = input_grads.astype(jnp.bfloat16)
    tap_grads = jnp.stack([lax.optimization_barrier(jnp.sum(grad_stack * padded[:, 2 - tap_lag:2 - tap_lag + length, :], axis=1)) for tap_lag in range(3)], axis=1) / math.sqrt(length)
    return (layer_out, input_grads, filter_grad, tap_grads)

def reference(query_in, key_in, value_in, grad_out, long_filter, short_taps):
    layer_out, input_grads, filter_grad, tap_grads = lax.map(one_section, (query_in, key_in, value_in, grad_out, long_filter, short_taps))
    passed_grads = jnp.concatenate([input_grads[1:], jnp.zeros_like(input_grads[:1])], axis=0)
    return (layer_out, passed_grads, filter_grad, tap_grads)
```

```python
import functools
import math

import jax
import jax.numpy as jnp
from jax import lax
from jax.experimental import pallas as pl
from jax.experimental.pallas import tpu as pltpu
from jax.sharding import PartitionSpec as P

f32 = jnp.float32
bf16 = jnp.bfloat16

N = 16
R = 128
C = 4096
Q = 4
CQ = C // Q
G = 16
OC = CQ // N
GQ = OC // G
T = N * R
W = 256
PARAMS = pltpu.CompilerParams(vmem_limit_bytes=56 * 2**20)


def rows_down(x, first):
    row = lax.broadcasted_iota(jnp.int32, x.shape, 0)
    return jnp.where(row == 0, first, pltpu.roll(x, 1, 0))


def rows_up(x, last):
    row = lax.broadcasted_iota(jnp.int32, x.shape, 0)
    return jnp.where(row == x.shape[0] - 1, last, pltpu.roll(x, x.shape[0] - 1, 0))


def short_filter(x, halo2, halo1, taps):
    back1 = rows_down(x, halo1)
    back2 = rows_down(back1, halo2)
    return taps[0] * x + taps[1] * back1 + taps[2] * back2


def features(lanes, in_refs, halo_ref, taps_ref):
    out = []
    for w in range(3):
        x = in_refs[w][:, lanes].astype(f32)
        taps = [taps_ref[3 * w + j : 3 * w + j + 1, lanes] for j in range(3)]
        out.append(
            short_filter(
                x, halo_ref[2 * w : 2 * w + 1, lanes], halo_ref[2 * w + 1 : 2 * w + 2, lanes], taps
            )
        )
    return out


def build_band(h, band_ref, base_ref, count):
    for r in range(8):
        base_ref[:, r, :] = h if r == 0 else pltpu.roll(h, r, 1)
    band_ref[:, :, 0:R] = jnp.zeros((count, R, R), bf16)

    def group(g, carry):
        base = base_ref[g]
        for m in range(R // 16):
            low = base if m == 0 else pltpu.roll(base, 16 * m, 1)
            high = pltpu.roll(base, 16 * m + 8, 1)
            both = jnp.concatenate([low, high], axis=0)
            row = lax.broadcasted_iota(jnp.int32, (16, R), 0) + 16 * m
            lane = lax.broadcasted_iota(jnp.int32, (16, R), 1)
            band_ref[g, 16 * m : 16 * m + 16, R : 2 * R] = jnp.where(
                lane >= row, both[:, :R], 0.0
            ).astype(bf16)
            band_ref[g, 16 * m : 16 * m + 16, 2 * R :] = both[:, R:].astype(bf16)
        return carry

    lax.fori_loop(0, count, group, 0)


def pair_lanes(x):
    v = x.reshape(N // 2, 2, G, R)
    return jnp.concatenate([v[:, 0], v[:, 1]], axis=-1).reshape(N // 2 * G, 2 * R)


def convolve(x, s, band):
    x2, s2 = pair_lanes(x), pair_lanes(s)
    zeros = jnp.zeros(((N // 2 - 1) * G, 2 * R), bf16)
    xp = jnp.concatenate([zeros, x2], axis=0)
    sp = jnp.concatenate([s2, zeros], axis=0)
    rows = N // 2 * G
    conv = back = None
    for d in range(N // 2):
        w = jnp.concatenate(
            [
                band[:, R + 2 * R * d : R + 2 * R * d + 2 * R],
                band[:, 2 * R * d : 2 * R * d + 2 * R],
            ],
            axis=0,
        )
        top = (N // 2 - 1 - d) * G
        c = jnp.dot(xp[top : top + rows], w, preferred_element_type=f32)
        b = lax.dot_general(
            sp[d * G : d * G + rows], w, (((1,), (1,)), ((), ())), preferred_element_type=f32
        )
        conv = c if conv is None else conv + c
        back = b if back is None else back + b
    return conv, back


def correlate(x, s, gram_ref):
    xt = x.reshape(N * G, R).astype(f32).T.astype(bf16)
    sp = jnp.concatenate([s.reshape(N * G, R), jnp.zeros((N * G, R), bf16)], axis=0)
    for d in range(N // 2):
        right = jnp.concatenate(
            [sp[2 * d * G : 2 * d * G + N * G], sp[(2 * d + 1) * G : (2 * d + 1) * G + N * G]],
            axis=1,
        )
        gram = jnp.dot(xt, right, preferred_element_type=f32)
        if d == 0:
            row = lax.broadcasted_iota(jnp.int32, gram.shape, 0)
            lane = lax.broadcasted_iota(jnp.int32, gram.shape, 1)
            gram = jnp.where(lane >= row, gram, 0.0)
        gram_ref[:, 2 * R * d : 2 * R * d + 2 * R] = gram
    total = gram_ref[0:8, :]
    for m in range(1, R // 8):
        total = total + pltpu.roll(gram_ref[8 * m : 8 * m + 8, :], T - 8 * m, 1)
    return total


def feature_kernel(q_ref, k_ref, v_ref, g_ref, halo_ref, taps_ref, out_ref):
    lanes = slice(None)
    query, keyed, valued = features(lanes, (q_ref, k_ref, v_ref), halo_ref, taps_ref)
    product = (keyed * valued).astype(bf16).astype(f32)
    scaled = (g_ref[...].astype(f32) * query).astype(bf16).astype(f32)
    for i in range(W // OC):
        out_ref[0, i, 0] = product.T[i * OC : (i + 1) * OC].astype(bf16)
        out_ref[0, i, 1] = scaled.T[i * OC : (i + 1) * OC].astype(bf16)


def conv_kernel(recv_ref, h_ref, ret_ref, fold_ref, band_ref, base_ref, gram_ref):
    build_band(h_ref[...], band_ref, base_ref, Q * GQ)

    def group(n, carry):
        q, i = n // GQ, n % GQ
        rows = pl.ds(pl.multiple_of(i * G, G), G)
        x = recv_ref[q, :, 0, rows, :]
        s = recv_ref[q, :, 1, rows, :]
        conv, back = convolve(x, s, band_ref.at[n])
        for w, value in ((0, conv), (1, back)):
            value = value.astype(bf16)
            for half in range(2):
                part = value[:, half * R : (half + 1) * R]
                for j in range(N // 2):
                    ret_ref[q, 2 * j + half, w, rows, :] = part[j * G : (j + 1) * G]
        fold_ref[n] = correlate(x, s, gram_ref)
        return carry

    lax.fori_loop(0, Q * GQ, group, 0)


def unfold(fold_ref):
    total = fold_ref[:, 0, :]
    for r in range(1, 8):
        total = total + pltpu.roll(fold_ref[:, r, :], T - r, 1)
    return total * (1.0 / math.sqrt(T * G))


def unfold_kernel(fold_ref, out_ref):
    out_ref[...] = unfold(fold_ref)


def grads_of(w, grad, conv, back, keyed, valued):
    return (grad * conv, back * valued, back * keyed)[w]


def finish_kernel(
    q_ref, k_ref, v_ref, g_ref, halo_ref, taps_ref, ret_ref, edge_ref, out_ref, grads_ref, tap_ref
):
    lanes = slice(None)
    query, keyed, valued = features(lanes, (q_ref, k_ref, v_ref), halo_ref, taps_ref)
    ret = ret_ref[0].astype(f32)
    conv = jnp.concatenate([ret[i, 0] for i in range(W // OC)], axis=0).T
    back = jnp.concatenate([ret[i, 1] for i in range(W // OC)], axis=0).T
    grad = g_ref[...].astype(f32)
    out_ref[...] = (query * conv).astype(bf16)
    raw = (q_ref, k_ref, v_ref)
    for w, g0 in enumerate((grad * conv, back * valued, back * keyed)):
        g1 = rows_up(g0, edge_ref[2 * w : 2 * w + 1, :])
        g2 = rows_up(g1, edge_ref[2 * w + 1 : 2 * w + 2, :])
        x = raw[w][...].astype(f32)
        total = None
        for j, g in enumerate((g0, g1, g2)):
            term = taps_ref[3 * w + j : 3 * w + j + 1, :] * g
            total = term if total is None else total + term
            tap_ref[3 * w + j : 3 * w + j + 1, :] = jnp.sum(g * x, axis=0, keepdims=True)
        grads_ref[w] = total.astype(bf16)


def edge_kernel(q_ref, k_ref, v_ref, g_ref, halo_ref, taps_ref, ret_ref, edge_ref):
    ret = ret_ref[0].astype(f32)
    conv = jnp.concatenate([ret[i, 0] for i in range(W // OC)], axis=0).T
    back = jnp.concatenate([ret[i, 1] for i in range(W // OC)], axis=0).T
    lanes = slice(None)
    query, keyed, valued = features(lanes, (q_ref, k_ref, v_ref), halo_ref, taps_ref)
    grad = g_ref[...].astype(f32)
    for w, g in enumerate((grad * conv, back * valued, back * keyed)):
        edge_ref[2 * w : 2 * w + 2, :] = g[0:2]
    edge_ref[6:8, :] = jnp.zeros((2, W), f32)


def passed(x, axis, by):
    count = lax.axis_size(axis)
    pairs = [(i, i + by) for i in range(count) if 0 <= i + by < count]
    return lax.ppermute(x, axis, pairs)


def exchange(x):
    return lax.all_to_all(x, "seq", split_axis=0, concat_axis=0, tiled=True)


def local(query_in, key_in, value_in, grad_out, long_filter, short_taps):
    raw = (query_in[0], key_in[0], value_in[0])
    grad = grad_out[0]
    taps = jnp.pad(short_taps[0].reshape(9, C), ((0, 7), (0, 0)))
    halo = passed(jnp.concatenate([x[R - 2 :] for x in raw], axis=0), "seq", 1)
    halo = jnp.pad(halo.astype(f32), ((0, 2), (0, 0)))
    turned = long_filter[0].T.reshape(Q, N, GQ, R).transpose(1, 0, 2, 3)
    h = exchange(turned).reshape(N, Q * GQ, R).transpose(1, 0, 2).reshape(Q * GQ, T)

    steps = C // W
    wide = lambda rows: pl.BlockSpec((rows, W), lambda n: (0, n))
    per = CQ // W
    owners = pl.BlockSpec(
        (1, W // OC, 2, OC, R), lambda n: (n // per, n % per, 0, 0, 0)
    )
    base_specs = [wide(R)] * 4 + [wide(8), wide(16)]
    sent = pl.pallas_call(
        feature_kernel,
        grid=(steps,),
        in_specs=base_specs,
        out_specs=owners,
        out_shape=jax.ShapeDtypeStruct((Q, N, 2, OC, R), bf16),
        compiler_params=PARAMS,
    )(*raw, grad, halo, taps)
    recv = lax.all_to_all(sent, "seq", split_axis=1, concat_axis=1, tiled=True)
    whole = pl.BlockSpec(memory_space=pltpu.VMEM)
    ret, fold = pl.pallas_call(
        conv_kernel,
        in_specs=[whole, whole],
        out_specs=[whole, whole],
        out_shape=[
            jax.ShapeDtypeStruct((Q, N, 2, OC, R), bf16),
            jax.ShapeDtypeStruct((Q * GQ, 8, T), f32),
        ],
        scratch_shapes=[
            pltpu.VMEM((Q * GQ, R, R + T), bf16),
            pltpu.VMEM((Q * GQ, 8, T), f32),
            pltpu.VMEM((R, T), f32),
        ],
        compiler_params=PARAMS,
    )(recv, h)
    ret = lax.all_to_all(ret, "seq", split_axis=1, concat_axis=1, tiled=True)
    unfolded = pl.pallas_call(
        unfold_kernel,
        in_specs=[whole],
        out_specs=whole,
        out_shape=jax.ShapeDtypeStruct((Q * GQ, T), f32),
        compiler_params=PARAMS,
    )(fold)
    pieces = exchange(unfolded.reshape(Q * GQ, N, R).transpose(1, 0, 2))
    filter_grad = pieces.reshape(N, Q, GQ, R).transpose(1, 0, 2, 3).reshape(C // G, R).T

    edge = pl.pallas_call(
        edge_kernel,
        grid=(steps,),
        in_specs=base_specs + [owners],
        out_specs=wide(8),
        out_shape=jax.ShapeDtypeStruct((8, C), f32),
        compiler_params=PARAMS,
    )(*raw, grad, halo, taps, ret)
    edge = passed(edge, "seq", -1)
    layer_out, input_grads, tap_sums = pl.pallas_call(
        finish_kernel,
        grid=(steps,),
        in_specs=base_specs + [owners, wide(8)],
        out_specs=[wide(R), pl.BlockSpec((3, R, W), lambda n: (0, 0, n)), wide(9)],
        out_shape=[
            jax.ShapeDtypeStruct((R, C), bf16),
            jax.ShapeDtypeStruct((3, R, C), bf16),
            jax.ShapeDtypeStruct((9, C), f32),
        ],
        compiler_params=PARAMS,
    )(*raw, grad, halo, taps, ret, edge)
    parts = exchange(tap_sums.reshape(9, N, C // N).transpose(1, 0, 2))
    owned = jnp.sum(parts, axis=0) * (1.0 / math.sqrt(T))
    tap_grads = exchange(jnp.broadcast_to(owned[None], (N, 9, C // N)))
    tap_grads = tap_grads.transpose(1, 0, 2).reshape(3, 3, C)
    passed_grads = passed(input_grads, "pipe", -1)
    return (layer_out[None], passed_grads[None], filter_grad[None], tap_grads[None])


def solution(mesh):
    in_specs = (
        P("pipe", "seq", None),
        P("pipe", "seq", None),
        P("pipe", "seq", None),
        P("pipe", "seq", None),
        P("pipe", "seq", None),
        P("pipe", None, None, None),
    )
    out_specs = (
        P("pipe", "seq", None),
        P("pipe", None, "seq", None),
        P("pipe", "seq", None),
        P("pipe", None, None, None),
    )
    return jax.shard_map(local, mesh=mesh, in_specs=in_specs, out_specs=out_specs, check_vma=False)
```

```python
import functools
import math

import jax
import jax.numpy as jnp
from jax import lax
from jax.experimental import pallas as pl
from jax.experimental.pallas import tpu as pltpu
from jax.sharding import PartitionSpec as P

f32 = jnp.float32
bf16 = jnp.bfloat16

N = 16
R = 128
C = 4096
Q = 4
CQ = C // Q
G = 16
OC = CQ // N
GQ = OC // G
T = N * R
W = 256
B = CQ // W


def rows_down(x, first):
    row = lax.broadcasted_iota(jnp.int32, x.shape, 0)
    return jnp.where(row == 0, first, pltpu.roll(x, 1, 0))


def rows_up(x, last):
    row = lax.broadcasted_iota(jnp.int32, x.shape, 0)
    return jnp.where(row == x.shape[0] - 1, last, pltpu.roll(x, x.shape[0] - 1, 0))


def short_filter(x, halo2, halo1, taps):
    back1 = rows_down(x, halo1)
    back2 = rows_down(back1, halo2)
    return taps[0] * x + taps[1] * back1 + taps[2] * back2


def features(lanes, in_refs, halo_ref, taps_ref):
    out = []
    for w in range(3):
        x = in_refs[w][:, lanes].astype(f32)
        taps = [taps_ref[w, j : j + 1, lanes] for j in range(3)]
        out.append(
            short_filter(
                x, halo_ref[2 * w : 2 * w + 1, lanes], halo_ref[2 * w + 1 : 2 * w + 2, lanes], taps
            )
        )
    return out


def build_band(h, band_ref, base_ref, count):
    for r in range(8):
        base_ref[:, r, :] = h if r == 0 else pltpu.roll(h, r, 1)
    band_ref[:, :, 0:R] = jnp.zeros((count, R, R), bf16)

    def group(g, carry):
        base = base_ref[g]
        for m in range(R // 16):
            low = base if m == 0 else pltpu.roll(base, 16 * m, 1)
            high = pltpu.roll(base, 16 * m + 8, 1)
            both = jnp.concatenate([low, high], axis=0)
            row = lax.broadcasted_iota(jnp.int32, (16, R), 0) + 16 * m
            lane = lax.broadcasted_iota(jnp.int32, (16, R), 1)
            band_ref[g, 16 * m : 16 * m + 16, R : 2 * R] = jnp.where(
                lane >= row, both[:, :R], 0.0
            ).astype(bf16)
            band_ref[g, 16 * m : 16 * m + 16, 2 * R :] = both[:, R:].astype(bf16)
        return carry

    lax.fori_loop(0, count, group, 0)


def pair_lanes(x):
    v = x.reshape(N // 2, 2, G, R)
    return jnp.concatenate([v[:, 0], v[:, 1]], axis=-1).reshape(N // 2 * G, 2 * R)


def convolve(x, s, band):
    x2, s2 = pair_lanes(x), pair_lanes(s)
    zeros = jnp.zeros(((N // 2 - 1) * G, 2 * R), bf16)
    xp = jnp.concatenate([zeros, x2], axis=0)
    sp = jnp.concatenate([s2, zeros], axis=0)
    rows = N // 2 * G
    conv = back = None
    for d in range(N // 2):
        w = jnp.concatenate(
            [
                band[:, R + 2 * R * d : R + 2 * R * d + 2 * R],
                band[:, 2 * R * d : 2 * R * d + 2 * R],
            ],
            axis=0,
        )
        top = (N // 2 - 1 - d) * G
        c = jnp.dot(xp[top : top + rows], w, preferred_element_type=f32)
        b = lax.dot_general(
            sp[d * G : d * G + rows], w, (((1,), (1,)), ((), ())), preferred_element_type=f32
        )
        conv = c if conv is None else conv + c
        back = b if back is None else back + b
    return conv, back


def correlate(x, s, gram_ref):
    xt = x.reshape(N * G, R).astype(f32).T.astype(bf16)
    sp = jnp.concatenate([s.reshape(N * G, R), jnp.zeros((N * G, R), bf16)], axis=0)
    for d in range(N // 2):
        right = jnp.concatenate(
            [sp[2 * d * G : 2 * d * G + N * G], sp[(2 * d + 1) * G : (2 * d + 1) * G + N * G]],
            axis=1,
        )
        gram = jnp.dot(xt, right, preferred_element_type=f32)
        if d == 0:
            row = lax.broadcasted_iota(jnp.int32, gram.shape, 0)
            lane = lax.broadcasted_iota(jnp.int32, gram.shape, 1)
            gram = jnp.where(lane >= row, gram, 0.0)
        gram_ref[:, 2 * R * d : 2 * R * d + 2 * R] = gram
    total = gram_ref[0:8, :]
    for m in range(1, R // 8):
        total = total + pltpu.roll(gram_ref[8 * m : 8 * m + 8, :], T - 8 * m, 1)
    return total


def block(n, size):
    return pl.ds(pl.multiple_of(n * size, size), size)


def whole_kernel(
    q_ref, k_ref, v_ref, g_ref, filter_ref, taps_ref,
    out_ref, passed_ref, fgrad_ref, tap_ref,
    feat, send, recv, ret_send, ret_recv, band, base, gram, fold, slabs, zeros,
    halo_out, halo_in, edge_out, edge_in, filt_out, filt_in, fg_out, fg_in, fg_rows,
    tap_out, tap_in, sum_out, sum_in,
    s_halo, r_halo, s_filt, r_filt, s_fwd, r_fwd, s_ret, r_ret, s_edge, r_edge,
    s_pipe, r_pipe, s_fg, r_fg, s_tap, r_tap, s_sum, r_sum, s_zero,
):
    me = lax.axis_index("seq")
    pipe = lax.axis_index("pipe")
    sections = lax.axis_size("pipe")
    raw = (q_ref, k_ref, v_ref)

    def peer_of(s):
        return lax.rem(me + s, N)

    def each_peer(fn):
        def step(s, carry):
            fn(peer_of(s))
            return carry

        lax.fori_loop(1, N, step, 0)

    def remote(src, dst, s_sem, r_sem, where):
        return pltpu.make_async_remote_copy(
            src_ref=src, dst_ref=dst, send_sem=s_sem, recv_sem=r_sem,
            device_id=where, device_id_type=pl.DeviceIdType.MESH,
        )

    def spread(src, dst, s_sem, r_sem):
        def start(k):
            remote(src.at[k], dst.at[me], s_sem.at[k], r_sem.at[me], {"seq": k}).start()

        def wait_recv(k):
            remote(src.at[k], dst.at[k], s_sem.at[k], r_sem.at[k], {"seq": k}).wait_recv()

        def wait_send(k):
            remote(src.at[k], dst.at[k], s_sem.at[k], r_sem.at[k], {"seq": k}).wait_send()

        return start, wait_recv, wait_send

    barrier = pltpu.get_barrier_semaphore()

    def greet(k):
        pl.semaphore_signal(
            barrier, inc=1, device_id={"seq": k}, device_id_type=pl.DeviceIdType.MESH
        )

    each_peer(greet)
    for by in (1, sections - 1):
        pl.semaphore_signal(
            barrier, inc=1, device_id={"pipe": lax.rem(pipe + by, sections)},
            device_id_type=pl.DeviceIdType.MESH,
        )

    for w in range(3):
        last = raw[w][R - 16 : R, :].astype(f32)
        halo_out[2 * w : 2 * w + 2, :] = last[14:16]
    halo_out[6:8, :] = jnp.zeros((2, C), f32)
    turned = filter_ref[...].T
    for k in range(N):
        for q in range(Q):
            first = q * N * GQ + k * GQ
            filt_out[k, q * GQ : (q + 1) * GQ, :] = turned[first : first + GQ]
    filt_in[me] = filt_out[me]

    pl.semaphore_wait(barrier, N + 1)

    def halo_copy():
        return remote(halo_out, halo_in, s_halo, r_halo, {"seq": jnp.minimum(me + 1, N - 1)})

    @pl.when(me < N - 1)
    def _():
        halo_copy().start()

    filt = spread(filt_out, filt_in, s_filt, r_filt)
    each_peer(filt[0])

    @pl.when(me == 0)
    def _():
        halo_in[...] = jnp.zeros_like(halo_in)

    @pl.when(me > 0)
    def _():
        halo_copy().wait_recv()

    fwd = [spread(send.at[q], recv.at[q], s_fwd.at[q], r_fwd.at[q]) for q in range(Q)]
    ret = [spread(ret_send.at[q], ret_recv.at[q], s_ret.at[q], r_ret.at[q]) for q in range(Q)]

    def feature_phase(q):
        def step(b, carry):
            n = q * B + b
            lanes = block(n, W)
            query, keyed, valued = features(lanes, raw, halo_in, taps_ref)
            feat[0, :, lanes] = query
            feat[1, :, lanes] = keyed
            feat[2, :, lanes] = valued
            product = (keyed * valued).astype(bf16).astype(f32).T
            scaled = (g_ref[:, lanes].astype(f32) * query).astype(bf16).astype(f32).T
            for i in range(W // OC):
                send[q, b * (W // OC) + i, 0] = product[i * OC : (i + 1) * OC].astype(bf16)
                send[q, b * (W // OC) + i, 1] = scaled[i * OC : (i + 1) * OC].astype(bf16)
            return carry

        lax.fori_loop(0, B, step, 0)
        each_peer(fwd[q][0])
        recv[q, me] = send[q, me]

    def conv_phase(q):
        each_peer(fwd[q][1])

        def group(i, carry):
            rows = block(i, G)
            conv, back = convolve(
                recv[q, :, 0, rows, :], recv[q, :, 1, rows, :], band.at[q * GQ + i]
            )
            for w, value in ((0, conv), (1, back)):
                value = value.astype(bf16)
                for half in range(2):
                    part = value[:, half * R : (half + 1) * R]
                    for j in range(N // 2):
                        ret_send[q, 2 * j + half, w, rows, :] = part[j * G : (j + 1) * G]
            return carry

        lax.fori_loop(0, GQ, group, 0)
        each_peer(ret[q][0])
        ret_recv[q, me] = ret_send[q, me]

    def corr_phase(q):
        def group(i, carry):
            rows = block(i, G)
            fold[q * GQ + i] = correlate(
                recv[q, :, 0, rows, :], recv[q, :, 1, rows, :], gram
            )
            return carry

        lax.fori_loop(0, GQ, group, 0)

    def edge_copy(q):
        return remote(
            edge_out.at[q], edge_in.at[q], s_edge.at[q], r_edge.at[q],
            {"seq": jnp.maximum(me - 1, 0)},
        )

    def grad_phase(q):
        each_peer(ret[q][1])

        def step(b, carry):
            lanes = block(q * B + b, W)
            owners = W // OC
            got = [
                jnp.concatenate(
                    [ret_recv[q, b * owners + i, w].astype(f32) for i in range(owners)], axis=0
                ).T
                for w in range(2)
            ]
            conv, back = got
            grad = g_ref[:, lanes].astype(f32)
            out_ref[:, lanes] = (feat[0, :, lanes] * conv).astype(bf16)
            grads = (grad * conv, back * feat[2, :, lanes], back * feat[1, :, lanes])
            for w in range(3):
                feat[w, :, lanes] = grads[w]
                edge_out[q, 2 * w : 2 * w + 2, block(b, W)] = grads[w][0:2]
            edge_out[q, 6:8, block(b, W)] = jnp.zeros((2, W), f32)
            return carry

        lax.fori_loop(0, B, step, 0)

        @pl.when(me > 0)
        def _():
            edge_copy(q).start()

        @pl.when(me == N - 1)
        def _():
            edge_in[q] = jnp.zeros((8, CQ), f32)

    tap_start, tap_wait_recv, tap_wait_send = spread(tap_out, tap_in, s_tap, r_tap)

    def pipe_copy(q):
        return remote(
            slabs.at[q], passed_ref.at[:, :, q * CQ : (q + 1) * CQ], s_pipe.at[q], r_pipe.at[q],
            {"pipe": jnp.maximum(pipe - 1, 0)},
        )

    def input_phase(q):
        @pl.when(me < N - 1)
        def _():
            edge_copy(q).wait_recv()

        def step(b, carry):
            n = q * B + b
            lanes = block(n, W)
            near = block(b, W)
            for w in range(3):
                g0 = feat[w, :, lanes]
                g1 = rows_up(g0, edge_in[q, 2 * w : 2 * w + 1, near])
                g2 = rows_up(g1, edge_in[q, 2 * w + 1 : 2 * w + 2, near])
                x = raw[w][:, lanes].astype(f32)
                total = None
                for j, g in enumerate((g0, g1, g2)):
                    term = taps_ref[w, j : j + 1, lanes] * g
                    total = term if total is None else total + term
                    tap_out[n, 3 * w + j : 3 * w + j + 1, :] = jnp.sum(g * x, axis=0, keepdims=True)
                slabs[q, w, :, near] = total.astype(bf16)

            @pl.when(n == me)
            def _():
                tap_in[n] = tap_out[n]

            @pl.when(n != me)
            def _():
                tap_start(n)

            return carry

        lax.fori_loop(0, B, step, 0)

        @pl.when(pipe > 0)
        def _():
            pipe_copy(q).start()

    def filter_phase():
        each_peer(filt[1])
        h = jnp.concatenate([filt_in[j] for j in range(N)], axis=1)
        build_band(h, band, base, Q * GQ)

    fg_start, fg_wait_recv, fg_wait_send = spread(fg_out, fg_in, s_fg, r_fg)

    def unfold_phase():
        total = fold[:, 0, :]
        for r in range(1, 8):
            total = total + pltpu.roll(fold[:, r, :], T - r, 1)
        total = total * (1.0 / math.sqrt(T * G))
        for k in range(N):
            fg_out[k] = total[:, k * R : (k + 1) * R]
        fg_in[me] = fg_out[me]
        each_peer(fg_start)

    def fgrad_phase():
        each_peer(fg_wait_recv)
        for k in range(N):
            for q in range(Q):
                first = q * N * GQ + k * GQ
                fg_rows[first : first + GQ, :] = fg_in[k, q * GQ : (q + 1) * GQ, :]
        fgrad_ref[...] = fg_rows[...].T

    def zero_copy():
        return pltpu.make_async_copy(zeros, passed_ref, s_zero)

    @pl.when(pipe == sections - 1)
    def _():
        zeros[...] = jnp.zeros_like(zeros)
        zero_copy().start()

    feature_phase(0)
    feature_phase(1)
    filter_phase()
    feature_phase(2)
    feature_phase(3)
    conv_phase(0)
    conv_phase(1)
    corr_phase(0)
    conv_phase(2)
    corr_phase(1)
    grad_phase(0)
    conv_phase(3)
    corr_phase(2)
    input_phase(0)
    grad_phase(1)
    corr_phase(3)
    unfold_phase()
    input_phase(1)
    grad_phase(2)
    input_phase(2)
    grad_phase(3)
    input_phase(3)

    each_peer(tap_wait_recv)
    owned = tap_in[0]
    for k in range(1, N):
        owned = owned + tap_in[k]
    sum_out[...] = owned * (1.0 / math.sqrt(T))
    sum_in[me] = sum_out[...]

    def sum_copy(k, slot):
        return remote(sum_out, sum_in.at[slot], s_sum.at[k], r_sum.at[slot], {"seq": k})

    each_peer(lambda k: sum_copy(k, me).start())
    fgrad_phase()
    each_peer(lambda k: sum_copy(k, k).wait_recv())
    for k in range(N):
        for w in range(3):
            tap_ref[w, :, k * W : (k + 1) * W] = sum_in[k, 3 * w : 3 * w + 3, :]

    @pl.when(me < N - 1)
    def _():
        halo_copy().wait_send()

    each_peer(filt[2])
    for q in range(Q):
        each_peer(fwd[q][2])
        each_peer(ret[q][2])
    each_peer(fg_wait_send)
    each_peer(tap_wait_send)
    each_peer(lambda k: sum_copy(k, k).wait_send())

    @pl.when(me > 0)
    def _():
        for q in range(Q):
            edge_copy(q).wait_send()

    @pl.when(pipe > 0)
    def _():
        for q in range(Q):
            pipe_copy(q).wait_send()

    @pl.when(pipe < sections - 1)
    def _():
        for q in range(Q):
            pipe_copy(q).wait_recv()

    @pl.when(pipe == sections - 1)
    def _():
        zero_copy().wait()


def local(query_in, key_in, value_in, grad_out, long_filter, short_taps):
    vmem = pl.BlockSpec(memory_space=pltpu.VMEM)
    hbm = pl.BlockSpec(memory_space=pl.ANY)
    dma = pltpu.SemaphoreType.DMA
    layer_out, passed_grads, filter_grad, tap_grads = pl.pallas_call(
        whole_kernel,
        in_specs=[vmem] * 6,
        out_specs=[vmem, hbm, vmem, vmem],
        out_shape=[
            jax.ShapeDtypeStruct((R, C), bf16),
            jax.ShapeDtypeStruct((3, R, C), bf16),
            jax.ShapeDtypeStruct((R, C // G), f32),
            jax.ShapeDtypeStruct((3, 3, C), f32),
        ],
        scratch_shapes=[
            pltpu.VMEM((3, R, C), f32),
            pltpu.VMEM((Q, N, 2, OC, R), bf16),
            pltpu.VMEM((Q, N, 2, OC, R), bf16),
            pltpu.VMEM((Q, N, 2, OC, R), bf16),
            pltpu.VMEM((Q, N, 2, OC, R), bf16),
            pltpu.VMEM((Q * GQ, R, R + T), bf16),
            pltpu.VMEM((Q * GQ, 8, T), f32),
            pltpu.VMEM((R, T), f32),
            pltpu.VMEM((Q * GQ, 8, T), f32),
            pltpu.VMEM((Q, 3, R, CQ), bf16),
            pltpu.VMEM((3, R, C), bf16),
            pltpu.VMEM((8, C), f32),
            pltpu.VMEM((8, C), f32),
            pltpu.VMEM((Q, 8, CQ), f32),
            pltpu.VMEM((Q, 8, CQ), f32),
            pltpu.VMEM((N, Q * GQ, R), f32),
            pltpu.VMEM((N, Q * GQ, R), f32),
            pltpu.VMEM((N, Q * GQ, R), f32),
            pltpu.VMEM((N, Q * GQ, R), f32),
            pltpu.VMEM((C // G, R), f32),
            pltpu.VMEM((N, 9, W), f32),
            pltpu.VMEM((N, 9, W), f32),
            pltpu.VMEM((9, W), f32),
            pltpu.VMEM((N, 9, W), f32),
            dma, dma,
            dma((N,)), dma((N,)),
            dma((Q, N)), dma((Q, N)),
            dma((Q, N)), dma((Q, N)),
            dma((Q,)), dma((Q,)),
            dma((Q,)), dma((Q,)),
            dma((N,)), dma((N,)),
            dma((N,)), dma((N,)),
            dma((N,)), dma((N,)),
            dma,
        ],
        compiler_params=pltpu.CompilerParams(
            collective_id=0, has_side_effects=True, vmem_limit_bytes=60 * 2**20
        ),
    )(query_in[0], key_in[0], value_in[0], grad_out[0], long_filter[0], short_taps[0])
    return (layer_out[None], passed_grads[None], filter_grad[None], tap_grads[None])


def solution(mesh):
    in_specs = (
        P("pipe", "seq", None),
        P("pipe", "seq", None),
        P("pipe", "seq", None),
        P("pipe", "seq", None),
        P("pipe", "seq", None),
        P("pipe", None, None, None),
    )
    out_specs = (
        P("pipe", "seq", None),
        P("pipe", None, "seq", None),
        P("pipe", "seq", None),
        P("pipe", None, None, None),
    )
    return jax.shard_map(local, mesh=mesh, in_specs=in_specs, out_specs=out_specs, check_vma=False)
```

```python
import functools
import math

import jax
import jax.numpy as jnp
from jax import lax
from jax.experimental import pallas as pl
from jax.experimental.pallas import tpu as pltpu
from jax.sharding import PartitionSpec as P

f32 = jnp.float32
bf16 = jnp.bfloat16

N = 16
R = 128
C = 4096
Q = 8
CQ = C // Q
G = 16
OC = CQ // N
GQ = OC // G
T = N * R
W = 256
B = CQ // W
HALVES = 2
TW = C // N // HALVES
AHEAD = 2
LAG = 1


def rows_down(x, first):
    row = lax.broadcasted_iota(jnp.int32, x.shape, 0)
    return jnp.where(row == 0, first, pltpu.roll(x, 1, 0))


def rows_up(x, last):
    row = lax.broadcasted_iota(jnp.int32, x.shape, 0)
    return jnp.where(row == x.shape[0] - 1, last, pltpu.roll(x, x.shape[0] - 1, 0))


def short_filter(x, halo2, halo1, taps):
    back1 = rows_down(x, halo1)
    back2 = rows_down(back1, halo2)
    return taps[0] * x + taps[1] * back1 + taps[2] * back2


def features(lanes, in_refs, halo_ref, taps_ref):
    out = []
    for w in range(3):
        x = in_refs[w][:, lanes].astype(f32)
        taps = [taps_ref[3 * w + j, :, lanes] for j in range(3)]
        out.append(
            short_filter(
                x, halo_ref[2 * w : 2 * w + 1, lanes], halo_ref[2 * w + 1 : 2 * w + 2, lanes], taps
            )
        )
    return out


def build_base(h, base_ref):
    for r in range(8):
        base_ref[:, r, :] = h if r == 0 else pltpu.roll(h, r, 1)


def build_band(base, band_ref):
    band_ref[:, 0:R] = jnp.zeros((R, R), bf16)
    for m in range(R // 16):
        low = base if m == 0 else pltpu.roll(base, 16 * m, 1)
        high = pltpu.roll(base, 16 * m + 8, 1)
        both = jnp.concatenate([low, high], axis=0)
        row = lax.broadcasted_iota(jnp.int32, (16, R), 0) + 16 * m
        lane = lax.broadcasted_iota(jnp.int32, (16, R), 1)
        rows = slice(16 * m, 16 * m + 16)
        band_ref[rows, R : 2 * R] = jnp.where(lane >= row, both[:, :R], 0.0).astype(bf16)
        band_ref[rows, 2 * R :] = both[:, R:].astype(bf16)


def pair_lanes(x):
    v = x.reshape(N // 2, 2, G, R)
    return jnp.concatenate([v[:, 0], v[:, 1]], axis=-1).reshape(N // 2 * G, 2 * R)


def convolve(x, s, band):
    x2, s2 = pair_lanes(x), pair_lanes(s)
    zeros = jnp.zeros(((N // 2 - 1) * G, 2 * R), bf16)
    xp = jnp.concatenate([zeros, x2], axis=0)
    sp = jnp.concatenate([s2, zeros], axis=0)
    rows = N // 2 * G
    conv = back = None
    for d in range(N // 2):
        w = jnp.concatenate(
            [
                band[:, R + 2 * R * d : R + 2 * R * d + 2 * R],
                band[:, 2 * R * d : 2 * R * d + 2 * R],
            ],
            axis=0,
        )
        top = (N // 2 - 1 - d) * G
        c = jnp.dot(xp[top : top + rows], w, preferred_element_type=f32)
        b = lax.dot_general(
            sp[d * G : d * G + rows], w, (((1,), (1,)), ((), ())), preferred_element_type=f32
        )
        conv = c if conv is None else conv + c
        back = b if back is None else back + b
    return conv, back


def correlate(x, s, gram_ref):
    xt = x.reshape(N * G, R).astype(f32).T.astype(bf16)
    sp = jnp.concatenate([s.reshape(N * G, R), jnp.zeros((N * G, R), bf16)], axis=0)
    for d in range(N // 2):
        right = jnp.concatenate(
            [sp[2 * d * G : 2 * d * G + N * G], sp[(2 * d + 1) * G : (2 * d + 1) * G + N * G]],
            axis=1,
        )
        gram = jnp.dot(xt, right, preferred_element_type=f32)
        if d == 0:
            row = lax.broadcasted_iota(jnp.int32, gram.shape, 0)
            lane = lax.broadcasted_iota(jnp.int32, gram.shape, 1)
            gram = jnp.where(lane >= row, gram, 0.0)
        gram_ref[:, 2 * R * d : 2 * R * d + 2 * R] = gram
    total = gram_ref[0:8, :]
    for m in range(1, R // 8):
        total = total + pltpu.roll(gram_ref[8 * m : 8 * m + 8, :], T - 8 * m, 1)
    return total


def block(n, size):
    return pl.ds(pl.multiple_of(n * size, size), size)


def whole_kernel(
    q_hbm, k_hbm, v_hbm, g_hbm, filter_ref, taps_ref,
    out_hbm, passed_ref, fgrad_ref, tap_ref,
    inputs, out_ref, feat, send, recv, ret_send, ret_recv, band, base, gram, fold, slabs, zeros,
    halo_out, halo_in, edge_out, edge_in, filt_pack, filt_out, filt_in, fg_out, fg_in, fg_rows,
    tap_out, tap_in, sum_out, sum_in,
    s_halo, r_halo, s_filt, r_filt, s_fwd, r_fwd, s_ret, r_ret, s_edge, r_edge,
    s_pipe, r_pipe, s_fg, r_fg, s_tap, r_tap, s_sum, r_sum, s_zero, s_in, s_out,
):
    me = lax.axis_index("seq")
    pipe = lax.axis_index("pipe")
    sections = lax.axis_size("pipe")
    raw = tuple(inputs.at[w] for w in range(3))
    g_ref = inputs.at[3]

    def load(w):
        return pltpu.make_async_copy((q_hbm, k_hbm, v_hbm, g_hbm)[w], inputs.at[w], s_in.at[w])

    for w in range(4):
        load(w).start()

    def peer_of(s):
        return lax.rem(me + s, N)

    def each_peer(fn):
        def step(s, carry):
            fn(peer_of(s))
            return carry

        lax.fori_loop(1, N, step, 0)

    def remote(src, dst, s_sem, r_sem, where):
        return pltpu.make_async_remote_copy(
            src_ref=src, dst_ref=dst, send_sem=s_sem, recv_sem=r_sem,
            device_id=where, device_id_type=pl.DeviceIdType.MESH,
        )

    def spread(src, dst, s_sem, r_sem):
        def start(k):
            remote(src.at[k], dst.at[me], s_sem.at[k], r_sem.at[me], {"seq": k}).start()

        def wait_recv(k):
            remote(src.at[k], dst.at[k], s_sem.at[k], r_sem.at[k], {"seq": k}).wait_recv()

        def wait_send(k):
            remote(src.at[k], dst.at[k], s_sem.at[k], r_sem.at[k], {"seq": k}).wait_send()

        return start, wait_recv, wait_send

    barrier = pltpu.get_barrier_semaphore()

    def greet(k):
        pl.semaphore_signal(
            barrier, inc=1, device_id={"seq": k}, device_id_type=pl.DeviceIdType.MESH
        )

    each_peer(greet)
    for by in (1, sections - 1):
        pl.semaphore_signal(
            barrier, inc=1, device_id={"pipe": lax.rem(pipe + by, sections)},
            device_id_type=pl.DeviceIdType.MESH,
        )

    for w in range(4):
        load(w).wait()
    for w in range(3):
        last = raw[w][R - 16 : R, :].astype(f32)
        halo_out[2 * w : 2 * w + 2, :] = last[14:16]
    halo_out[6:8, :] = jnp.zeros((2, C), f32)
    turned = filter_ref[...].T
    for k in range(N):
        for q in range(Q):
            first = q * N * GQ + k * GQ
            filt_pack[k, q * GQ : (q + 1) * GQ, :] = turned[first : first + GQ]
    filt_out[...] = filt_pack[...].astype(bf16)
    filt_in[me] = filt_out[me]

    pl.semaphore_wait(barrier, N + 1)

    def halo_copy(q):
        lanes = block(q, CQ)
        return remote(
            halo_out.at[:, lanes], halo_in.at[:, lanes], s_halo.at[q], r_halo.at[q],
            {"seq": jnp.minimum(me + 1, N - 1)},
        )

    @pl.when(me < N - 1)
    def _():
        for q in range(Q):
            halo_copy(q).start()

    filt = spread(filt_out, filt_in, s_filt, r_filt)
    each_peer(filt[0])

    @pl.when(me == 0)
    def _():
        halo_in[...] = jnp.zeros_like(halo_in)

    def fwd(q):
        return spread(send.at[q], recv.at[q], s_fwd.at[q], r_fwd.at[q])

    def ret(q):
        return spread(ret_send.at[q], ret_recv.at[q], s_ret.at[q], r_ret.at[q])

    def feature_phase(q):
        @pl.when(me > 0)
        def _():
            halo_copy(q).wait_recv()

        def step(b, carry):
            n = q * B + b
            lanes = block(n, W)
            query, keyed, valued = features(lanes, raw, halo_in, taps_ref)
            feat[0, :, lanes] = query
            feat[1, :, lanes] = keyed
            feat[2, :, lanes] = valued
            product = (keyed * valued).astype(bf16).astype(f32).T
            scaled = (g_ref[:, lanes].astype(f32) * query).astype(bf16).astype(f32).T
            for i in range(W // OC):
                send[q, b * (W // OC) + i, 0] = product[i * OC : (i + 1) * OC].astype(bf16)
                send[q, b * (W // OC) + i, 1] = scaled[i * OC : (i + 1) * OC].astype(bf16)
            return carry

        lax.fori_loop(0, B, step, 0)
        each_peer(fwd(q)[0])
        recv[q, me] = send[q, me]

    def band_phase(q):
        def group(i, carry):
            build_band(base[q * GQ + i], band.at[q * GQ + i])
            return carry

        lax.fori_loop(0, GQ, group, 0)

    def conv_phase(q):
        each_peer(fwd(q)[1])

        def group(i, carry):
            rows = block(i, G)
            conv, back = convolve(
                recv[q, :, 0, rows, :], recv[q, :, 1, rows, :], band.at[q * GQ + i]
            )
            for w, value in ((0, conv), (1, back)):
                value = value.astype(bf16)
                for half in range(2):
                    part = value[:, half * R : (half + 1) * R]
                    for j in range(N // 2):
                        ret_send[q, 2 * j + half, w, rows, :] = part[j * G : (j + 1) * G]
            return carry

        lax.fori_loop(0, GQ, group, 0)
        each_peer(ret(q)[0])
        ret_recv[q, me] = ret_send[q, me]

    def corr_phase(q):
        def group(i, carry):
            rows = block(i, G)
            fold[q * GQ + i] = correlate(
                recv[q, :, 0, rows, :], recv[q, :, 1, rows, :], gram
            )
            return carry

        lax.fori_loop(0, GQ, group, 0)

    def edge_copy(q):
        return remote(
            edge_out.at[q], edge_in.at[q], s_edge.at[q], r_edge.at[q],
            {"seq": jnp.maximum(me - 1, 0)},
        )

    def out_copy(q):
        lanes = block(q, CQ)
        return pltpu.make_async_copy(out_ref.at[:, lanes], out_hbm.at[:, lanes], s_out.at[q])

    def grad_phase(q):
        each_peer(ret(q)[1])

        def step(b, carry):
            lanes = block(q * B + b, W)
            owners = W // OC
            got = [
                jnp.concatenate(
                    [ret_recv[q, b * owners + i, w].astype(f32) for i in range(owners)], axis=0
                ).T
                for w in range(2)
            ]
            conv, back = got
            grad = g_ref[:, lanes].astype(f32)
            out_ref[:, lanes] = (feat[0, :, lanes] * conv).astype(bf16)
            grads = (grad * conv, back * feat[2, :, lanes], back * feat[1, :, lanes])
            for w in range(3):
                feat[w, :, lanes] = grads[w]
                edge_out[q, 2 * w : 2 * w + 2, block(b, W)] = grads[w][0:2]
            edge_out[q, 6:8, block(b, W)] = jnp.zeros((2, W), f32)
            return carry

        lax.fori_loop(0, B, step, 0)

        out_copy(q).start()

        @pl.when(me > 0)
        def _():
            edge_copy(q).start()

        @pl.when(me == N - 1)
        def _():
            edge_in[q] = jnp.zeros((8, CQ), f32)

    def tap(half):
        return spread(tap_out.at[half], tap_in.at[half], s_tap.at[half], r_tap.at[half])

    def pipe_copy(q):
        return remote(
            slabs.at[q], passed_ref.at[:, :, block(q, CQ)], s_pipe.at[q], r_pipe.at[q],
            {"pipe": jnp.maximum(pipe - 1, 0)},
        )

    def input_phase(q):
        @pl.when(me < N - 1)
        def _():
            edge_copy(q).wait_recv()

        def step(b, carry):
            n = q * B + b
            lanes = block(n, W)
            near = block(b, W)
            for w in range(3):
                g0 = feat[w, :, lanes]
                g1 = rows_up(g0, edge_in[q, 2 * w : 2 * w + 1, near])
                g2 = rows_up(g1, edge_in[q, 2 * w + 1 : 2 * w + 2, near])
                x = raw[w][:, lanes].astype(f32)
                total = None
                for j, g in enumerate((g0, g1, g2)):
                    term = taps_ref[3 * w + j, :, lanes] * g
                    total = term if total is None else total + term
                    part = jnp.sum(g * x, axis=0, keepdims=True)
                    for i in range(W // TW):
                        owner = lax.rem(n * (W // TW) + i, N)
                        half = lax.div(n * (W // TW), N)
                        tap_out[half, owner, 3 * w + j : 3 * w + j + 1, :] = part[:, i * TW : (i + 1) * TW]
                slabs[q, w, :, near] = total.astype(bf16)
            return carry

        lax.fori_loop(0, B, step, 0)

        @pl.when(pipe > 0)
        def _():
            pipe_copy(q).start()

        for half in range(HALVES):

            @pl.when(q == (half + 1) * (Q // HALVES) - 1)
            def _():
                each_peer(tap(half)[0])
                tap_in[half, me] = tap_out[half, me]

    def filter_phase():
        each_peer(filt[1])
        h = jnp.concatenate([filt_in[j].astype(f32) for j in range(N)], axis=1)
        build_base(h, base)

    fg_start, fg_wait_recv, fg_wait_send = spread(fg_out, fg_in, s_fg, r_fg)

    def unfold_phase():
        total = fold[:, 0, :]
        for r in range(1, 8):
            total = total + pltpu.roll(fold[:, r, :], T - r, 1)
        total = total * (1.0 / math.sqrt(T * G))
        for k in range(N):
            fg_out[k] = total[:, k * R : (k + 1) * R]
        fg_in[me] = fg_out[me]
        each_peer(fg_start)

    def fgrad_phase():
        each_peer(fg_wait_recv)
        for k in range(N):
            for q in range(Q):
                first = q * N * GQ + k * GQ
                fg_rows[first : first + GQ, :] = fg_in[k, q * GQ : (q + 1) * GQ, :]
        fgrad_ref[...] = fg_rows[...].T

    def zero_copy():
        return pltpu.make_async_copy(zeros, passed_ref, s_zero)

    def sum_copy(half, k, slot):
        return remote(
            sum_out.at[half], sum_in.at[half, slot], s_sum.at[half, k], r_sum.at[half, slot], {"seq": k}
        )

    def sum_phase(half):
        each_peer(tap(half)[1])
        owned = tap_in[half, 0]
        for k in range(1, N):
            owned = owned + tap_in[half, k]
        sum_out[half] = owned * (1.0 / math.sqrt(T))
        sum_in[half, me] = sum_out[half]
        each_peer(lambda k: sum_copy(half, k, me).start())

    for q in range(AHEAD):
        feature_phase(q)
    def zero_phase():
        @pl.when(pipe == sections - 1)
        def _():
            zeros[...] = jnp.zeros_like(zeros)
            zero_copy().start()

    filter_phase()
    band_phase(0)

    def step(t, carry):
        @pl.when(t < Q)
        def _():
            conv_phase(t)

        @pl.when(t + AHEAD < Q)
        def _():
            feature_phase(t + AHEAD)

        @pl.when((t >= LAG) & (t < Q + LAG))
        def _():
            grad_phase(t - LAG)

        @pl.when(t + 1 < Q)
        def _():
            band_phase(t + 1)

        @pl.when(t < Q)
        def _():
            corr_phase(t)

        @pl.when(t == Q - 1)
        def _():
            unfold_phase()

        @pl.when(t == 0)
        def _():
            zero_phase()

        @pl.when(t >= LAG + 1)
        def _():
            input_phase(t - LAG - 1)

        @pl.when(t == Q // HALVES + LAG + 1)
        def _():
            sum_phase(0)

        return carry

    lax.fori_loop(0, Q + LAG + 1, step, 0)

    sum_phase(1)
    fgrad_phase()
    for half in range(HALVES):
        each_peer(lambda k: sum_copy(half, k, k).wait_recv())
        for k in range(N):
            first = half * (C // HALVES) + k * TW
            for r in range(9):
                tap_ref[r, :, first : first + TW] = sum_in[half, k, r : r + 1, :]

    @pl.when(me < N - 1)
    def _():
        for q in range(Q):
            halo_copy(q).wait_send()

    each_peer(filt[2])

    def sent(q, carry):
        each_peer(fwd(q)[2])
        each_peer(ret(q)[2])
        out_copy(q).wait()
        return carry

    lax.fori_loop(0, Q, sent, 0)
    each_peer(fg_wait_send)
    for half in range(HALVES):
        each_peer(tap(half)[2])
        each_peer(lambda k: sum_copy(half, k, k).wait_send())

    @pl.when(me > 0)
    def _():
        for q in range(Q):
            edge_copy(q).wait_send()

    @pl.when(pipe > 0)
    def _():
        for q in range(Q):
            pipe_copy(q).wait_send()

    @pl.when(pipe < sections - 1)
    def _():
        for q in range(Q):
            pipe_copy(q).wait_recv()

    @pl.when(pipe == sections - 1)
    def _():
        zero_copy().wait()


def copy_kernel(out_in, passed_in, fgrad_in, tap_in, out, passed, fgrad, tap):
    out[...] = out_in[...]
    passed[...] = passed_in[...]
    fgrad[...] = fgrad_in[...]
    tap[...] = tap_in[...]


def local(query_in, key_in, value_in, grad_out, long_filter, short_taps):
    vmem = pl.BlockSpec(memory_space=pltpu.VMEM)
    hbm = pl.BlockSpec(memory_space=pl.ANY)
    dma = pltpu.SemaphoreType.DMA
    layer_out, passed_grads, filter_grad, tap_grads = pl.pallas_call(
        whole_kernel,
        in_specs=[hbm] * 4 + [vmem] * 2,
        out_specs=[hbm, hbm, vmem, vmem],
        out_shape=[
            jax.ShapeDtypeStruct((R, C), bf16),
            jax.ShapeDtypeStruct((3, R, C), bf16),
            jax.ShapeDtypeStruct((R, C // G), f32),
            jax.ShapeDtypeStruct((9, 1, C), f32),
        ],
        scratch_shapes=[
            pltpu.VMEM((4, R, C), bf16),
            pltpu.VMEM((R, C), bf16),
            pltpu.VMEM((3, R, C), f32),
            pltpu.VMEM((Q, N, 2, OC, R), bf16),
            pltpu.VMEM((Q, N, 2, OC, R), bf16),
            pltpu.VMEM((Q, N, 2, OC, R), bf16),
            pltpu.VMEM((Q, N, 2, OC, R), bf16),
            pltpu.VMEM((Q * GQ, R, R + T), bf16),
            pltpu.VMEM((Q * GQ, 8, T), f32),
            pltpu.VMEM((R, T), f32),
            pltpu.VMEM((Q * GQ, 8, T), f32),
            pltpu.VMEM((Q, 3, R, CQ), bf16),
            pltpu.VMEM((3, R, C), bf16),
            pltpu.VMEM((8, C), f32),
            pltpu.VMEM((8, C), f32),
            pltpu.VMEM((Q, 8, CQ), f32),
            pltpu.VMEM((Q, 8, CQ), f32),
            pltpu.VMEM((N, Q * GQ, R), f32),
            pltpu.VMEM((N, Q * GQ, R), bf16),
            pltpu.VMEM((N, Q * GQ, R), bf16),
            pltpu.VMEM((N, Q * GQ, R), f32),
            pltpu.VMEM((N, Q * GQ, R), f32),
            pltpu.VMEM((C // G, R), f32),
            pltpu.VMEM((HALVES, N, 9, TW), f32),
            pltpu.VMEM((HALVES, N, 9, TW), f32),
            pltpu.VMEM((HALVES, 9, TW), f32),
            pltpu.VMEM((HALVES, N, 9, TW), f32),
            dma((Q,)), dma((Q,)),
            dma((N,)), dma((N,)),
            dma((Q, N)), dma((Q, N)),
            dma((Q, N)), dma((Q, N)),
            dma((Q,)), dma((Q,)),
            dma((Q,)), dma((Q,)),
            dma((N,)), dma((N,)),
            dma((HALVES, N)), dma((HALVES, N)),
            dma((HALVES, N)), dma((HALVES, N)),
            dma,
            dma((4,)),
            dma((Q,)),
        ],
        compiler_params=pltpu.CompilerParams(
            collective_id=0, has_side_effects=True, vmem_limit_bytes=60 * 2**20
        ),
    )(query_in[0], key_in[0], value_in[0], grad_out[0], long_filter[0],
      short_taps[0].reshape(9, 1, C))
    specs = [
        pl.BlockSpec((R // 4, C), lambda n: (n, 0)),
        pl.BlockSpec((3, R // 4, C), lambda n: (0, n, 0)),
        pl.BlockSpec((R // 4, C // G), lambda n: (n, 0)),
        pl.BlockSpec((9, 1, C // 4), lambda n: (0, 0, n)),
    ]
    layer_out, passed_grads, filter_grad, tap_grads = pl.pallas_call(
        copy_kernel,
        grid=(4,),
        in_specs=specs,
        out_specs=specs,
        out_shape=[
            jax.ShapeDtypeStruct((R, C), bf16),
            jax.ShapeDtypeStruct((3, R, C), bf16),
            jax.ShapeDtypeStruct((R, C // G), f32),
            jax.ShapeDtypeStruct((9, 1, C), f32),
        ],
    )(layer_out, passed_grads, filter_grad, tap_grads)
    tap_grads = tap_grads.reshape(1, 3, 3, C)
    return (layer_out[None], passed_grads[None], filter_grad[None], tap_grads)


def solution(mesh):
    in_specs = (
        P("pipe", "seq", None),
        P("pipe", "seq", None),
        P("pipe", "seq", None),
        P("pipe", "seq", None),
        P("pipe", "seq", None),
        P("pipe", None, None, None),
    )
    out_specs = (
        P("pipe", "seq", None),
        P("pipe", None, "seq", None),
        P("pipe", "seq", None),
        P("pipe", None, None, None),
    )
    return jax.shard_map(local, mesh=mesh, in_specs=in_specs, out_specs=out_specs, check_vma=False)
```

```python
import functools
import math

import jax
import jax.numpy as jnp
from jax import lax
from jax.experimental import pallas as pl
from jax.experimental.pallas import tpu as pltpu
from jax.sharding import PartitionSpec as P

f32 = jnp.float32
bf16 = jnp.bfloat16

N = 16
R = 128
C = 4096
Q = 8
CQ = C // Q
G = 16
OC = CQ // N
GQ = OC // G
T = N * R
W = 256
B = CQ // W
HALVES = 2
TW = C // N // HALVES
AHEAD = 2
LAG = 1


def rows_down(x, first):
    row = lax.broadcasted_iota(jnp.int32, x.shape, 0)
    return jnp.where(row == 0, first, pltpu.roll(x, 1, 0))


def rows_up(x, last):
    row = lax.broadcasted_iota(jnp.int32, x.shape, 0)
    return jnp.where(row == x.shape[0] - 1, last, pltpu.roll(x, x.shape[0] - 1, 0))


def short_filter(x, halo2, halo1, taps):
    back1 = rows_down(x, halo1)
    back2 = rows_down(back1, halo2)
    return taps[0] * x + taps[1] * back1 + taps[2] * back2


def features(lanes, in_refs, halo, taps_ref):
    out = []
    for w in range(3):
        x = in_refs[w][:, lanes].astype(f32)
        taps = [taps_ref[3 * w + j, :, lanes] for j in range(3)]
        out.append(short_filter(x, halo[2 * w : 2 * w + 1], halo[2 * w + 1 : 2 * w + 2], taps))
    return out


def eight_rows(ref, b):
    rows = ref[...].astype(f32)
    return jnp.where(b == 0, rows[0:8], rows[8:16])


def build_base(h, base_ref):
    for r in range(8):
        base_ref[:, r, :] = h if r == 0 else pltpu.roll(h, r, 1)


def build_band(base, band_ref):
    band_ref[:, 0:R] = jnp.zeros((R, R), bf16)
    for m in range(R // 16):
        low = base if m == 0 else pltpu.roll(base, 16 * m, 1)
        high = pltpu.roll(base, 16 * m + 8, 1)
        both = jnp.concatenate([low, high], axis=0)
        row = lax.broadcasted_iota(jnp.int32, (16, R), 0) + 16 * m
        lane = lax.broadcasted_iota(jnp.int32, (16, R), 1)
        rows = slice(16 * m, 16 * m + 16)
        band_ref[rows, R : 2 * R] = jnp.where(lane >= row, both[:, :R], 0.0).astype(bf16)
        band_ref[rows, 2 * R :] = both[:, R:].astype(bf16)


def pair_lanes(x):
    v = x.reshape(N // 2, 2, G, R)
    return jnp.concatenate([v[:, 0], v[:, 1]], axis=-1).reshape(N // 2 * G, 2 * R)


def convolve(x, s, band):
    x2, s2 = pair_lanes(x), pair_lanes(s)
    zeros = jnp.zeros(((N // 2 - 1) * G, 2 * R), bf16)
    xp = jnp.concatenate([zeros, x2], axis=0)
    sp = jnp.concatenate([s2, zeros], axis=0)
    rows = N // 2 * G
    conv = back = None
    for d in range(N // 2):
        w = jnp.concatenate(
            [
                band[:, R + 2 * R * d : R + 2 * R * d + 2 * R],
                band[:, 2 * R * d : 2 * R * d + 2 * R],
            ],
            axis=0,
        )
        top = (N // 2 - 1 - d) * G
        c = jnp.dot(xp[top : top + rows], w, preferred_element_type=f32)
        b = lax.dot_general(
            sp[d * G : d * G + rows], w, (((1,), (1,)), ((), ())), preferred_element_type=f32
        )
        conv = c if conv is None else conv + c
        back = b if back is None else back + b
    return conv, back


def correlate(x, s, gram_ref):
    xt = x.reshape(N * G, R).astype(f32).T.astype(bf16)
    sp = jnp.concatenate([s.reshape(N * G, R), jnp.zeros((N * G, R), bf16)], axis=0)
    for d in range(N // 2):
        right = jnp.concatenate(
            [sp[2 * d * G : 2 * d * G + N * G], sp[(2 * d + 1) * G : (2 * d + 1) * G + N * G]],
            axis=1,
        )
        gram = jnp.dot(xt, right, preferred_element_type=f32)
        if d == 0:
            row = lax.broadcasted_iota(jnp.int32, gram.shape, 0)
            lane = lax.broadcasted_iota(jnp.int32, gram.shape, 1)
            gram = jnp.where(lane >= row, gram, 0.0)
        gram_ref[:, 2 * R * d : 2 * R * d + 2 * R] = gram
    total = gram_ref[0:8, :]
    for m in range(1, R // 8):
        total = total + pltpu.roll(gram_ref[8 * m : 8 * m + 8, :], T - 8 * m, 1)
    return total


def block(n, size):
    return pl.ds(pl.multiple_of(n * size, size), size)


def whole_kernel(
    q_hbm, k_hbm, v_hbm, g_hbm, filter_ref, taps_ref,
    out_hbm, passed_ref, fgrad_ref, tap_ref,
    inputs, out_ref, feat, send, recv, ret_send, ret_recv, band, base, gram, fold, slabs, zeros,
    halo_pack, halo_out, halo_in, edge_pack, edge_out, edge_in, filt_pack, filt_out, filt_in, fg_out, fg_in, fg_rows,
    tap_out, tap_in, sum_out, sum_in,
    s_halo, r_halo, s_filt, r_filt, s_fwd, r_fwd, s_ret, r_ret, s_edge, r_edge,
    s_pipe, r_pipe, s_fg, r_fg, s_tap, r_tap, s_sum, r_sum, s_zero, s_in, s_out,
):
    me = lax.axis_index("seq")
    pipe = lax.axis_index("pipe")
    sections = lax.axis_size("pipe")
    raw = tuple(inputs.at[w] for w in range(3))
    g_ref = inputs.at[3]

    def load(w):
        return pltpu.make_async_copy((q_hbm, k_hbm, v_hbm, g_hbm)[w], inputs.at[w], s_in.at[w])

    for w in range(4):
        load(w).start()

    def peer_of(s):
        half = lax.div(s + 1, 2)
        return lax.rem(me + N + half * (2 * lax.rem(s, 2) - 1), N)

    def each_peer(fn):
        def step(s, carry):
            fn(peer_of(s))
            return carry

        lax.fori_loop(1, N, step, 0)

    def remote(src, dst, s_sem, r_sem, where):
        return pltpu.make_async_remote_copy(
            src_ref=src, dst_ref=dst, send_sem=s_sem, recv_sem=r_sem,
            device_id=where, device_id_type=pl.DeviceIdType.MESH,
        )

    def spread(src, dst, s_sem, r_sem):
        def start(k):
            remote(src.at[k], dst.at[me], s_sem.at[k], r_sem.at[me], {"seq": k}).start()

        def wait_recv(k):
            remote(src.at[k], dst.at[k], s_sem.at[k], r_sem.at[k], {"seq": k}).wait_recv()

        def wait_send(k):
            remote(src.at[k], dst.at[k], s_sem.at[k], r_sem.at[k], {"seq": k}).wait_send()

        return start, wait_recv, wait_send

    barrier = pltpu.get_barrier_semaphore()

    def greet(k):
        pl.semaphore_signal(
            barrier, inc=1, device_id={"seq": k}, device_id_type=pl.DeviceIdType.MESH
        )

    each_peer(greet)
    for by in (1, sections - 1):
        pl.semaphore_signal(
            barrier, inc=1, device_id={"pipe": lax.rem(pipe + by, sections)},
            device_id_type=pl.DeviceIdType.MESH,
        )

    for w in range(4):
        load(w).wait()
    halo_pack[...] = jnp.zeros_like(halo_pack)
    for w in range(3):
        last = raw[w][R - 16 : R, :].astype(f32)[14:16]
        for q in range(Q):
            for b in range(B):
                first = q * CQ + b * W
                halo_pack[q, 8 * b + 2 * w : 8 * b + 2 * w + 2, :] = last[:, first : first + W]
    halo_out[...] = halo_pack[...].astype(bf16)

    pl.semaphore_wait(barrier, N + 1)

    def halo_copy(q):
        return remote(
            halo_out.at[q], halo_in.at[q], s_halo.at[q], r_halo.at[q],
            {"seq": jnp.minimum(me + 1, N - 1)},
        )

    @pl.when(me < N - 1)
    def _():
        for q in range(Q):
            halo_copy(q).start()

    turned = filter_ref[...].T
    for k in range(N):
        for q in range(Q):
            first = q * N * GQ + k * GQ
            filt_pack[k, q * GQ : (q + 1) * GQ, :] = turned[first : first + GQ]
    filt_out[...] = filt_pack[...].astype(bf16)
    filt_in[me] = filt_out[me]
    filt = spread(filt_out, filt_in, s_filt, r_filt)
    each_peer(filt[0])

    @pl.when(me == 0)
    def _():
        halo_in[...] = jnp.zeros_like(halo_in)

    def fwd(q):
        return spread(send.at[q], recv.at[q], s_fwd.at[q], r_fwd.at[q])

    def ret(q):
        return spread(ret_send.at[q], ret_recv.at[q], s_ret.at[q], r_ret.at[q])

    def feature_phase(q):
        @pl.when(me > 0)
        def _():
            halo_copy(q).wait_recv()

        def step(b, carry):
            n = q * B + b
            lanes = block(n, W)
            query, keyed, valued = features(lanes, raw, eight_rows(halo_in.at[q], b), taps_ref)
            feat[0, :, lanes] = query
            feat[1, :, lanes] = keyed
            feat[2, :, lanes] = valued
            product = (keyed * valued).astype(bf16).astype(f32).T
            scaled = (g_ref[:, lanes].astype(f32) * query).astype(bf16).astype(f32).T
            for i in range(W // OC):
                send[q, b * (W // OC) + i, 0] = product[i * OC : (i + 1) * OC].astype(bf16)
                send[q, b * (W // OC) + i, 1] = scaled[i * OC : (i + 1) * OC].astype(bf16)
            return carry

        lax.fori_loop(0, B, step, 0)
        each_peer(fwd(q)[0])
        recv[q, me] = send[q, me]

    def band_phase(q):
        def group(i, carry):
            build_band(base[q * GQ + i], band.at[q * GQ + i])
            return carry

        lax.fori_loop(0, GQ, group, 0)

    def conv_phase(q):
        each_peer(fwd(q)[1])

        def group(i, carry):
            rows = block(i, G)
            conv, back = convolve(
                recv[q, :, 0, rows, :], recv[q, :, 1, rows, :], band.at[q * GQ + i]
            )
            for w, value in ((0, conv), (1, back)):
                value = value.astype(bf16)
                for half in range(2):
                    part = value[:, half * R : (half + 1) * R]
                    for j in range(N // 2):
                        ret_send[q, 2 * j + half, w, rows, :] = part[j * G : (j + 1) * G]
            return carry

        lax.fori_loop(0, GQ, group, 0)
        each_peer(ret(q)[0])
        ret_recv[q, me] = ret_send[q, me]

    def corr_phase(q):
        def group(i, carry):
            rows = block(i, G)
            fold[q * GQ + i] = correlate(
                recv[q, :, 0, rows, :], recv[q, :, 1, rows, :], gram
            )
            return carry

        lax.fori_loop(0, GQ, group, 0)

    def edge_copy(q):
        return remote(
            edge_out.at[q], edge_in.at[q], s_edge.at[q], r_edge.at[q],
            {"seq": jnp.maximum(me - 1, 0)},
        )

    def out_copy(q):
        lanes = block(q, CQ)
        return pltpu.make_async_copy(out_ref.at[:, lanes], out_hbm.at[:, lanes], s_out.at[q])

    def grad_phase(q):
        each_peer(ret(q)[1])

        def step(b, carry):
            lanes = block(q * B + b, W)
            owners = W // OC
            got = [
                jnp.concatenate(
                    [ret_recv[q, b * owners + i, w].astype(f32) for i in range(owners)], axis=0
                ).T
                for w in range(2)
            ]
            conv, back = got
            grad = g_ref[:, lanes].astype(f32)
            out_ref[:, lanes] = (feat[0, :, lanes] * conv).astype(bf16)
            grads = (grad * conv, back * feat[2, :, lanes], back * feat[1, :, lanes])
            for w in range(3):
                feat[w, :, lanes] = grads[w]
            rows = [g[0:2] for g in grads] + [jnp.zeros((2, W), f32)]
            edge_pack[block(b, 8), :] = jnp.concatenate(rows, axis=0)
            return carry

        lax.fori_loop(0, B, step, 0)
        edge_out[q] = edge_pack[...].astype(bf16)

        out_copy(q).start()

        @pl.when(me > 0)
        def _():
            edge_copy(q).start()

        @pl.when(me == N - 1)
        def _():
            edge_in[q] = jnp.zeros((16, W), bf16)

    def tap(half):
        return spread(tap_out.at[half], tap_in.at[half], s_tap.at[half], r_tap.at[half])

    def pipe_copy(q):
        return remote(
            slabs.at[q], passed_ref.at[:, :, block(q, CQ)], s_pipe.at[q], r_pipe.at[q],
            {"pipe": jnp.maximum(pipe - 1, 0)},
        )

    def input_phase(q):
        @pl.when(me < N - 1)
        def _():
            edge_copy(q).wait_recv()

        def step(b, carry):
            n = q * B + b
            lanes = block(n, W)
            near = block(b, W)
            edge = eight_rows(edge_in.at[q], b)
            for w in range(3):
                g0 = feat[w, :, lanes]
                g1 = rows_up(g0, edge[2 * w : 2 * w + 1])
                g2 = rows_up(g1, edge[2 * w + 1 : 2 * w + 2])
                x = raw[w][:, lanes].astype(f32)
                total = None
                for j, g in enumerate((g0, g1, g2)):
                    term = taps_ref[3 * w + j, :, lanes] * g
                    total = term if total is None else total + term
                    part = jnp.sum(g * x, axis=0, keepdims=True)
                    for i in range(W // TW):
                        owner = lax.rem(n * (W // TW) + i, N)
                        half = lax.div(n * (W // TW), N)
                        tap_out[half, owner, 3 * w + j : 3 * w + j + 1, :] = part[:, i * TW : (i + 1) * TW]
                slabs[q, w, :, near] = total.astype(bf16)
            return carry

        lax.fori_loop(0, B, step, 0)

        @pl.when(pipe > 0)
        def _():
            pipe_copy(q).start()

        for half in range(HALVES):

            @pl.when(q == (half + 1) * (Q // HALVES) - 1)
            def _():
                each_peer(tap(half)[0])
                tap_in[half, me] = tap_out[half, me]

    def filter_phase():
        each_peer(filt[1])
        h = jnp.concatenate([filt_in[j].astype(f32) for j in range(N)], axis=1)
        build_base(h, base)

    fg_start, fg_wait_recv, fg_wait_send = spread(fg_out, fg_in, s_fg, r_fg)

    def unfold_phase():
        total = fold[:, 0, :]
        for r in range(1, 8):
            total = total + pltpu.roll(fold[:, r, :], T - r, 1)
        total = total * (1.0 / math.sqrt(T * G))
        for k in range(N):
            fg_out[k] = total[:, k * R : (k + 1) * R]
        fg_in[me] = fg_out[me]
        each_peer(fg_start)

    def fgrad_phase():
        each_peer(fg_wait_recv)
        for k in range(N):
            for q in range(Q):
                first = q * N * GQ + k * GQ
                fg_rows[first : first + GQ, :] = fg_in[k, q * GQ : (q + 1) * GQ, :]
        fgrad_ref[...] = fg_rows[...].T

    def zero_copy():
        return pltpu.make_async_copy(zeros, passed_ref, s_zero)

    def sum_copy(half, k, slot):
        return remote(
            sum_out.at[half], sum_in.at[half, slot], s_sum.at[half, k], r_sum.at[half, slot], {"seq": k}
        )

    def sum_phase(half):
        each_peer(tap(half)[1])
        owned = tap_in[half, 0]
        for k in range(1, N):
            owned = owned + tap_in[half, k]
        sum_out[half] = owned * (1.0 / math.sqrt(T))
        sum_in[half, me] = sum_out[half]
        each_peer(lambda k: sum_copy(half, k, me).start())

    for q in range(AHEAD):
        feature_phase(q)
    def zero_phase():
        @pl.when(pipe == sections - 1)
        def _():
            zeros[...] = jnp.zeros_like(zeros)
            zero_copy().start()

    filter_phase()
    band_phase(0)

    def step(t, carry):
        @pl.when(t < Q)
        def _():
            conv_phase(t)

        @pl.when(t + AHEAD < Q)
        def _():
            feature_phase(t + AHEAD)

        @pl.when((t >= LAG) & (t < Q + LAG))
        def _():
            grad_phase(t - LAG)

        @pl.when(t + 1 < Q)
        def _():
            band_phase(t + 1)

        @pl.when(t < Q)
        def _():
            corr_phase(t)

        @pl.when(t == Q - 1)
        def _():
            unfold_phase()

        @pl.when(t == 0)
        def _():
            zero_phase()

        @pl.when(t >= LAG + 1)
        def _():
            input_phase(t - LAG - 1)

        @pl.when(t == Q // HALVES + LAG + 1)
        def _():
            sum_phase(0)

        return carry

    lax.fori_loop(0, Q + LAG + 1, step, 0)

    def sent(q, carry):
        each_peer(fwd(q)[2])
        each_peer(ret(q)[2])
        out_copy(q).wait()
        return carry

    fgrad_phase()
    lax.fori_loop(0, Q // 2, sent, 0)
    sum_phase(1)
    lax.fori_loop(Q // 2, Q, sent, 0)

    @pl.when(me < N - 1)
    def _():
        for q in range(Q):
            halo_copy(q).wait_send()

    each_peer(filt[2])
    each_peer(fg_wait_send)
    for half in range(HALVES):
        each_peer(tap(half)[2])
        each_peer(lambda k: sum_copy(half, k, k).wait_send())

    for half in range(HALVES):
        each_peer(lambda k: sum_copy(half, k, k).wait_recv())
        for r in range(9):
            tap_ref[r, half * N : (half + 1) * N, :] = sum_in[half, :, r, :]

    @pl.when(me > 0)
    def _():
        for q in range(Q):
            edge_copy(q).wait_send()

    @pl.when(pipe > 0)
    def _():
        for q in range(Q):
            pipe_copy(q).wait_send()

    @pl.when(pipe < sections - 1)
    def _():
        for q in range(Q):
            pipe_copy(q).wait_recv()

    @pl.when(pipe == sections - 1)
    def _():
        zero_copy().wait()


def copy_kernel(
    out_in, passed_in, fgrad_in, tap_in, out, passed, fgrad, tap, v_out, v_passed, v_fgrad, v_tap, sem
):
    pairs = []
    for n in range(4):
        rows = slice(n * R // 4, (n + 1) * R // 4)
        pairs += [(passed_in.at[w, rows], v_passed.at[w, rows], passed.at[w, rows]) for w in range(3)]
        pairs.append((out_in.at[rows], v_out.at[rows], out.at[rows]))
    pairs += [(fgrad_in, v_fgrad, fgrad), (tap_in, v_tap, tap)]
    into = [pltpu.make_async_copy(a, b, sem.at[0, i]) for i, (a, b, _) in enumerate(pairs)]
    back = [pltpu.make_async_copy(b, c, sem.at[1, i]) for i, (_, b, c) in enumerate(pairs)]
    for copy in into:
        copy.start()
    for first, second in zip(into, back):
        first.wait()
        second.start()
    for copy in back:
        copy.wait()


def local(query_in, key_in, value_in, grad_out, long_filter, short_taps):
    vmem = pl.BlockSpec(memory_space=pltpu.VMEM)
    hbm = pl.BlockSpec(memory_space=pl.ANY)
    dma = pltpu.SemaphoreType.DMA
    layer_out, passed_grads, filter_grad, tap_grads = pl.pallas_call(
        whole_kernel,
        in_specs=[hbm] * 4 + [vmem] * 2,
        out_specs=[hbm, hbm, vmem, vmem],
        out_shape=[
            jax.ShapeDtypeStruct((R, C), bf16),
            jax.ShapeDtypeStruct((3, R, C), bf16),
            jax.ShapeDtypeStruct((R, C // G), f32),
            jax.ShapeDtypeStruct((9, C // TW, TW), f32),
        ],
        scratch_shapes=[
            pltpu.VMEM((4, R, C), bf16),
            pltpu.VMEM((R, C), bf16),
            pltpu.VMEM((3, R, C), f32),
            pltpu.VMEM((Q, N, 2, OC, R), bf16),
            pltpu.VMEM((Q, N, 2, OC, R), bf16),
            pltpu.VMEM((Q, N, 2, OC, R), bf16),
            pltpu.VMEM((Q, N, 2, OC, R), bf16),
            pltpu.VMEM((Q * GQ, R, R + T), bf16),
            pltpu.VMEM((Q * GQ, 8, T), f32),
            pltpu.VMEM((R, T), f32),
            pltpu.VMEM((Q * GQ, 8, T), f32),
            pltpu.VMEM((Q, 3, R, CQ), bf16),
            pltpu.VMEM((3, R, C), bf16),
            pltpu.VMEM((Q, 16, W), f32),
            pltpu.VMEM((Q, 16, W), bf16),
            pltpu.VMEM((Q, 16, W), bf16),
            pltpu.VMEM((16, W), f32),
            pltpu.VMEM((Q, 16, W), bf16),
            pltpu.VMEM((Q, 16, W), bf16),
            pltpu.VMEM((N, Q * GQ, R), f32),
            pltpu.VMEM((N, Q * GQ, R), bf16),
            pltpu.VMEM((N, Q * GQ, R), bf16),
            pltpu.VMEM((N, Q * GQ, R), f32),
            pltpu.VMEM((N, Q * GQ, R), f32),
            pltpu.VMEM((C // G, R), f32),
            pltpu.VMEM((HALVES, N, 9, TW), f32),
            pltpu.VMEM((HALVES, N, 9, TW), f32),
            pltpu.VMEM((HALVES, 9, TW), f32),
            pltpu.VMEM((HALVES, N, 9, TW), f32),
            dma((Q,)), dma((Q,)),
            dma((N,)), dma((N,)),
            dma((Q, N)), dma((Q, N)),
            dma((Q, N)), dma((Q, N)),
            dma((Q,)), dma((Q,)),
            dma((Q,)), dma((Q,)),
            dma((N,)), dma((N,)),
            dma((HALVES, N)), dma((HALVES, N)),
            dma((HALVES, N)), dma((HALVES, N)),
            dma,
            dma((4,)),
            dma((Q,)),
        ],
        compiler_params=pltpu.CompilerParams(
            collective_id=0, has_side_effects=True, vmem_limit_bytes=60 * 2**20
        ),
    )(query_in[0], key_in[0], value_in[0], grad_out[0], long_filter[0],
      short_taps[0].reshape(9, 1, C))
    layer_out, passed_grads, filter_grad, tap_grads = pl.pallas_call(
        copy_kernel,
        in_specs=[hbm] * 4,
        out_specs=[hbm] * 4,
        out_shape=[
            jax.ShapeDtypeStruct((R, C), bf16),
            jax.ShapeDtypeStruct((3, R, C), bf16),
            jax.ShapeDtypeStruct((R, C // G), f32),
            jax.ShapeDtypeStruct((9, C // TW, TW), f32),
        ],
        scratch_shapes=[
            pltpu.VMEM((R, C), bf16),
            pltpu.VMEM((3, R, C), bf16),
            pltpu.VMEM((R, C // G), f32),
            pltpu.VMEM((9, C // TW, TW), f32),
            dma((2, 18)),
        ],
        compiler_params=pltpu.CompilerParams(vmem_limit_bytes=60 * 2**20),
    )(layer_out, passed_grads, filter_grad, tap_grads)
    tap_grads = tap_grads.reshape(1, 3, 3, C)
    return (layer_out[None], passed_grads[None], filter_grad[None], tap_grads)


def solution(mesh):
    in_specs = (
        P("pipe", "seq", None),
        P("pipe", "seq", None),
        P("pipe", "seq", None),
        P("pipe", "seq", None),
        P("pipe", "seq", None),
        P("pipe", None, None, None),
    )
    out_specs = (
        P("pipe", "seq", None),
        P("pipe", None, "seq", None),
        P("pipe", "seq", None),
        P("pipe", None, None, None),
    )
    return jax.shard_map(local, mesh=mesh, in_specs=in_specs, out_specs=out_specs, check_vma=False)
```

```python
import functools
import math

import jax
import jax.numpy as jnp
from jax import lax
from jax.experimental import pallas as pl
from jax.experimental.pallas import tpu as pltpu
from jax.sharding import PartitionSpec as P

f32 = jnp.float32
bf16 = jnp.bfloat16

N = 16
R = 128
C = 4096
Q = 8
CQ = C // Q
G = 16
OC = CQ // N
GQ = OC // G
T = N * R
W = 256
B = CQ // W
HALVES = 2
TW = C // N // HALVES
AHEAD = 2
LAG = 1


def rows_down(x, first):
    row = lax.broadcasted_iota(jnp.int32, x.shape, 0)
    return jnp.where(row == 0, first, pltpu.roll(x, 1, 0))


def rows_up(x, last):
    row = lax.broadcasted_iota(jnp.int32, x.shape, 0)
    return jnp.where(row == x.shape[0] - 1, last, pltpu.roll(x, x.shape[0] - 1, 0))


def short_filter(x, halo2, halo1, taps):
    back1 = rows_down(x, halo1)
    back2 = rows_down(back1, halo2)
    return taps[0] * x + taps[1] * back1 + taps[2] * back2


def features(lanes, in_refs, halo, taps_ref):
    out = []
    for w in range(3):
        x = in_refs[w][:, lanes].astype(f32)
        taps = [taps_ref[3 * w + j, :, lanes] for j in range(3)]
        out.append(short_filter(x, halo[2 * w : 2 * w + 1], halo[2 * w + 1 : 2 * w + 2], taps))
    return out


def eight_rows(ref, b):
    rows = ref[...].astype(f32)
    return jnp.where(b == 0, rows[0:8], rows[8:16])


def build_base(h, base_ref):
    for r in range(8):
        base_ref[:, r, :] = h if r == 0 else pltpu.roll(h, r, 1)


def build_band(base, band_ref):
    band_ref[:, 0:R] = jnp.zeros((R, R), bf16)
    for m in range(R // 16):
        low = base if m == 0 else pltpu.roll(base, 16 * m, 1)
        high = pltpu.roll(base, 16 * m + 8, 1)
        both = jnp.concatenate([low, high], axis=0)
        row = lax.broadcasted_iota(jnp.int32, (16, R), 0) + 16 * m
        lane = lax.broadcasted_iota(jnp.int32, (16, R), 1)
        rows = slice(16 * m, 16 * m + 16)
        band_ref[rows, R : 2 * R] = jnp.where(lane >= row, both[:, :R], 0.0).astype(bf16)
        band_ref[rows, 2 * R :] = both[:, R:].astype(bf16)


def pair_lanes(x):
    v = x.reshape(N // 2, 2, G, R)
    return jnp.concatenate([v[:, 0], v[:, 1]], axis=-1).reshape(N // 2 * G, 2 * R)


def convolve(x, s, band):
    x2, s2 = pair_lanes(x), pair_lanes(s)
    zeros = jnp.zeros(((N // 2 - 1) * G, 2 * R), bf16)
    xp = jnp.concatenate([zeros, x2], axis=0)
    sp = jnp.concatenate([s2, zeros], axis=0)
    rows = N // 2 * G
    conv = back = None
    for d in range(N // 2):
        w = jnp.concatenate(
            [
                band[:, R + 2 * R * d : R + 2 * R * d + 2 * R],
                band[:, 2 * R * d : 2 * R * d + 2 * R],
            ],
            axis=0,
        )
        top = (N // 2 - 1 - d) * G
        c = jnp.dot(xp[top : top + rows], w, preferred_element_type=f32)
        b = lax.dot_general(
            sp[d * G : d * G + rows], w, (((1,), (1,)), ((), ())), preferred_element_type=f32
        )
        conv = c if conv is None else conv + c
        back = b if back is None else back + b
    return conv, back


def correlate(x, s, gram_ref):
    xt = x.reshape(N * G, R).astype(f32).T.astype(bf16)
    sp = jnp.concatenate([s.reshape(N * G, R), jnp.zeros((N * G, R), bf16)], axis=0)
    for d in range(N // 2):
        right = jnp.concatenate(
            [sp[2 * d * G : 2 * d * G + N * G], sp[(2 * d + 1) * G : (2 * d + 1) * G + N * G]],
            axis=1,
        )
        gram = jnp.dot(xt, right, preferred_element_type=f32)
        if d == 0:
            row = lax.broadcasted_iota(jnp.int32, gram.shape, 0)
            lane = lax.broadcasted_iota(jnp.int32, gram.shape, 1)
            gram = jnp.where(lane >= row, gram, 0.0)
        gram_ref[:, 2 * R * d : 2 * R * d + 2 * R] = gram
    total = gram_ref[0:8, :]
    for m in range(1, R // 8):
        total = total + pltpu.roll(gram_ref[8 * m : 8 * m + 8, :], T - 8 * m, 1)
    return total


def block(n, size):
    return pl.ds(pl.multiple_of(n * size, size), size)


def whole_kernel(
    q_hbm, k_hbm, v_hbm, g_hbm, filter_ref, taps_ref,
    out_hbm, passed_ref, fgrad_ref, tap_ref,
    inputs, out_ref, feat, send, recv, ret_send, ret_recv, band, base, gram, fold, slabs, zeros,
    halo_pack, halo_out, halo_in, edge_pack, edge_out, edge_in, filt_pack, filt_out, filt_in, fg_out, fg_in, fg_rows,
    tap_out, tap_in, sum_out, sum_in,
    s_halo, r_halo, s_filt, r_filt, s_fwd, r_fwd, s_ret, r_ret, s_edge, r_edge,
    s_pipe, r_pipe, s_fg, r_fg, s_tap, r_tap, s_sum, r_sum, s_zero, s_in, s_out,
):
    me = lax.axis_index("seq")
    pipe = lax.axis_index("pipe")
    sections = lax.axis_size("pipe")
    raw = tuple(inputs.at[w] for w in range(3))
    g_ref = inputs.at[3]

    def load(w):
        return pltpu.make_async_copy((q_hbm, k_hbm, v_hbm, g_hbm)[w], inputs.at[w], s_in.at[w])

    for w in range(4):
        load(w).start()

    def peer_of(s):
        half = lax.div(s + 1, 2)
        return lax.rem(me + N + half * (2 * lax.rem(s, 2) - 1), N)

    def each_peer(fn):
        def step(s, carry):
            fn(peer_of(s))
            return carry

        lax.fori_loop(1, N, step, 0, unroll=True)

    def remote(src, dst, s_sem, r_sem, where):
        return pltpu.make_async_remote_copy(
            src_ref=src, dst_ref=dst, send_sem=s_sem, recv_sem=r_sem,
            device_id=where, device_id_type=pl.DeviceIdType.MESH,
        )

    def spread(src, dst, s_sem, r_sem):
        def start(k):
            remote(src.at[k], dst.at[me], s_sem.at[k], r_sem.at[me], {"seq": k}).start()

        def wait_recv(k):
            remote(src.at[k], dst.at[k], s_sem.at[k], r_sem.at[k], {"seq": k}).wait_recv()

        def wait_send(k):
            remote(src.at[k], dst.at[k], s_sem.at[k], r_sem.at[k], {"seq": k}).wait_send()

        return start, wait_recv, wait_send

    barrier = pltpu.get_barrier_semaphore()

    def greet(k):
        pl.semaphore_signal(
            barrier, inc=1, device_id={"seq": k}, device_id_type=pl.DeviceIdType.MESH
        )

    each_peer(greet)
    for by in (1, sections - 1):
        pl.semaphore_signal(
            barrier, inc=1, device_id={"pipe": lax.rem(pipe + by, sections)},
            device_id_type=pl.DeviceIdType.MESH,
        )

    for w in range(4):
        load(w).wait()
    halo_pack[...] = jnp.zeros_like(halo_pack)
    for w in range(3):
        last = raw[w][R - 16 : R, :].astype(f32)[14:16]
        for q in range(Q):
            for b in range(B):
                first = q * CQ + b * W
                halo_pack[q, 8 * b + 2 * w : 8 * b + 2 * w + 2, :] = last[:, first : first + W]
    halo_out[...] = halo_pack[...].astype(bf16)

    pl.semaphore_wait(barrier, N + 1)

    def halo_copy(q):
        return remote(
            halo_out.at[q], halo_in.at[q], s_halo.at[q], r_halo.at[q],
            {"seq": jnp.minimum(me + 1, N - 1)},
        )

    @pl.when(me < N - 1)
    def _():
        for q in range(Q):
            halo_copy(q).start()

    turned = filter_ref[...].T
    for k in range(N):
        for q in range(Q):
            first = q * N * GQ + k * GQ
            filt_pack[k, q * GQ : (q + 1) * GQ, :] = turned[first : first + GQ]
    filt_out[...] = filt_pack[...].astype(bf16)
    filt_in[me] = filt_out[me]
    filt = spread(filt_out, filt_in, s_filt, r_filt)
    each_peer(filt[0])

    @pl.when(me == 0)
    def _():
        halo_in[...] = jnp.zeros_like(halo_in)

    def fwd(q):
        return spread(send.at[q], recv.at[q], s_fwd.at[q], r_fwd.at[q])

    def ret(q):
        return spread(ret_send.at[q], ret_recv.at[q], s_ret.at[q], r_ret.at[q])

    def feature_phase(q):
        @pl.when(me > 0)
        def _():
            halo_copy(q).wait_recv()

        def step(b, carry):
            n = q * B + b
            lanes = block(n, W)
            query, keyed, valued = features(lanes, raw, eight_rows(halo_in.at[q], b), taps_ref)
            feat[0, :, lanes] = query
            feat[1, :, lanes] = keyed
            feat[2, :, lanes] = valued
            product = (keyed * valued).astype(bf16).astype(f32).T
            scaled = (g_ref[:, lanes].astype(f32) * query).astype(bf16).astype(f32).T
            for i in range(W // OC):
                send[q, b * (W // OC) + i, 0] = product[i * OC : (i + 1) * OC].astype(bf16)
                send[q, b * (W // OC) + i, 1] = scaled[i * OC : (i + 1) * OC].astype(bf16)
            return carry

        lax.fori_loop(0, B, step, 0)
        each_peer(fwd(q)[0])
        recv[q, me] = send[q, me]

    def band_phase(q):
        def group(i, carry):
            build_band(base[q * GQ + i], band.at[q * GQ + i])
            return carry

        lax.fori_loop(0, GQ, group, 0)

    def conv_phase(q):
        each_peer(fwd(q)[1])

        def group(i, carry):
            rows = block(i, G)
            conv, back = convolve(
                recv[q, :, 0, rows, :], recv[q, :, 1, rows, :], band.at[q * GQ + i]
            )
            for w, value in ((0, conv), (1, back)):
                value = value.astype(bf16)
                for half in range(2):
                    part = value[:, half * R : (half + 1) * R]
                    for j in range(N // 2):
                        ret_send[q, 2 * j + half, w, rows, :] = part[j * G : (j + 1) * G]
            return carry

        lax.fori_loop(0, GQ, group, 0)
        each_peer(ret(q)[0])
        ret_recv[q, me] = ret_send[q, me]

    def corr_phase(q):
        def group(i, carry):
            rows = block(i, G)
            fold[q * GQ + i] = correlate(
                recv[q, :, 0, rows, :], recv[q, :, 1, rows, :], gram
            )
            return carry

        lax.fori_loop(0, GQ, group, 0)

    def edge_copy(q):
        return remote(
            edge_out.at[q], edge_in.at[q], s_edge.at[q], r_edge.at[q],
            {"seq": jnp.maximum(me - 1, 0)},
        )

    def out_copy(q):
        lanes = block(q, CQ)
        return pltpu.make_async_copy(out_ref.at[:, lanes], out_hbm.at[:, lanes], s_out.at[q])

    def grad_phase(q):
        each_peer(ret(q)[1])

        def step(b, carry):
            lanes = block(q * B + b, W)
            owners = W // OC
            got = [
                jnp.concatenate(
                    [ret_recv[q, b * owners + i, w].astype(f32) for i in range(owners)], axis=0
                ).T
                for w in range(2)
            ]
            conv, back = got
            grad = g_ref[:, lanes].astype(f32)
            out_ref[:, lanes] = (feat[0, :, lanes] * conv).astype(bf16)
            grads = (grad * conv, back * feat[2, :, lanes], back * feat[1, :, lanes])
            for w in range(3):
                feat[w, :, lanes] = grads[w]
            rows = [g[0:2] for g in grads] + [jnp.zeros((2, W), f32)]
            edge_pack[block(b, 8), :] = jnp.concatenate(rows, axis=0)
            return carry

        lax.fori_loop(0, B, step, 0)
        edge_out[q] = edge_pack[...].astype(bf16)

        out_copy(q).start()

        @pl.when(me > 0)
        def _():
            edge_copy(q).start()

        @pl.when(me == N - 1)
        def _():
            edge_in[q] = jnp.zeros((16, W), bf16)

    def tap(half):
        return spread(tap_out.at[half], tap_in.at[half], s_tap.at[half], r_tap.at[half])

    def pipe_copy(q):
        return remote(
            slabs.at[q], passed_ref.at[:, :, block(q, CQ)], s_pipe.at[q], r_pipe.at[q],
            {"pipe": jnp.maximum(pipe - 1, 0)},
        )

    def input_phase(q):
        @pl.when(me < N - 1)
        def _():
            edge_copy(q).wait_recv()

        def step(b, carry):
            n = q * B + b
            lanes = block(n, W)
            near = block(b, W)
            edge = eight_rows(edge_in.at[q], b)
            for w in range(3):
                g0 = feat[w, :, lanes]
                g1 = rows_up(g0, edge[2 * w : 2 * w + 1])
                g2 = rows_up(g1, edge[2 * w + 1 : 2 * w + 2])
                x = raw[w][:, lanes].astype(f32)
                total = None
                for j, g in enumerate((g0, g1, g2)):
                    term = taps_ref[3 * w + j, :, lanes] * g
                    total = term if total is None else total + term
                    part = jnp.sum(g * x, axis=0, keepdims=True)
                    for i in range(W // TW):
                        owner = lax.rem(n * (W // TW) + i, N)
                        half = lax.div(n * (W // TW), N)
                        tap_out[half, owner, 3 * w + j : 3 * w + j + 1, :] = part[:, i * TW : (i + 1) * TW]
                slabs[q, w, :, near] = total.astype(bf16)
            return carry

        lax.fori_loop(0, B, step, 0)

        @pl.when(pipe > 0)
        def _():
            pipe_copy(q).start()

        for half in range(HALVES):

            @pl.when(q == (half + 1) * (Q // HALVES) - 1)
            def _():
                each_peer(tap(half)[0])
                tap_in[half, me] = tap_out[half, me]

    def filter_phase():
        each_peer(filt[1])
        h = jnp.concatenate([filt_in[j].astype(f32) for j in range(N)], axis=1)
        build_base(h, base)

    fg_start, fg_wait_recv, fg_wait_send = spread(fg_out, fg_in, s_fg, r_fg)

    def unfold_phase():
        total = fold[:, 0, :]
        for r in range(1, 8):
            total = total + pltpu.roll(fold[:, r, :], T - r, 1)
        total = total * (1.0 / math.sqrt(T * G))
        for k in range(N):
            fg_out[k] = total[:, k * R : (k + 1) * R]
        fg_in[me] = fg_out[me]
        each_peer(fg_start)

    def fgrad_phase():
        each_peer(fg_wait_recv)
        for k in range(N):
            for q in range(Q):
                first = q * N * GQ + k * GQ
                fg_rows[first : first + GQ, :] = fg_in[k, q * GQ : (q + 1) * GQ, :]
        fgrad_ref[...] = fg_rows[...].T

    def zero_copy():
        return pltpu.make_async_copy(zeros, passed_ref, s_zero)

    def sum_copy(half, k, slot):
        return remote(
            sum_out.at[half], sum_in.at[half, slot], s_sum.at[half, k], r_sum.at[half, slot], {"seq": k}
        )

    def sum_phase(half):
        each_peer(tap(half)[1])
        owned = tap_in[half, 0]
        for k in range(1, N):
            owned = owned + tap_in[half, k]
        sum_out[half] = owned * (1.0 / math.sqrt(T))
        sum_in[half, me] = sum_out[half]
        each_peer(lambda k: sum_copy(half, k, me).start())

    for q in range(AHEAD):
        feature_phase(q)
    def zero_phase():
        @pl.when(pipe == sections - 1)
        def _():
            zeros[...] = jnp.zeros_like(zeros)
            zero_copy().start()

    filter_phase()
    band_phase(0)

    def step(t, carry):
        @pl.when(t < Q)
        def _():
            conv_phase(t)

        @pl.when(t + AHEAD < Q)
        def _():
            feature_phase(t + AHEAD)

        @pl.when((t >= LAG) & (t < Q + LAG))
        def _():
            grad_phase(t - LAG)

        @pl.when(t + 1 < Q)
        def _():
            band_phase(t + 1)

        @pl.when(t < Q)
        def _():
            corr_phase(t)

        @pl.when(t == Q - 1)
        def _():
            unfold_phase()

        @pl.when(t == 0)
        def _():
            zero_phase()

        @pl.when(t >= LAG + 1)
        def _():
            input_phase(t - LAG - 1)

        @pl.when(t == Q)
        def _():
            sum_phase(0)

        return carry

    lax.fori_loop(0, Q + LAG + 1, step, 0)

    def sent(q, carry):
        each_peer(fwd(q)[2])
        each_peer(ret(q)[2])
        out_copy(q).wait()
        return carry

    fgrad_phase()
    lax.fori_loop(0, Q // 2, sent, 0)
    sum_phase(1)
    lax.fori_loop(Q // 2, Q, sent, 0)

    @pl.when(me < N - 1)
    def _():
        for q in range(Q):
            halo_copy(q).wait_send()

    each_peer(filt[2])
    each_peer(fg_wait_send)
    for half in range(HALVES):
        each_peer(tap(half)[2])
        each_peer(lambda k: sum_copy(half, k, k).wait_send())

    for half in range(HALVES):
        each_peer(lambda k: sum_copy(half, k, k).wait_recv())
        for r in range(9):
            tap_ref[r, half * N : (half + 1) * N, :] = sum_in[half, :, r, :]

    @pl.when(me > 0)
    def _():
        for q in range(Q):
            edge_copy(q).wait_send()

    @pl.when(pipe > 0)
    def _():
        for q in range(Q):
            pipe_copy(q).wait_send()

    @pl.when(pipe < sections - 1)
    def _():
        for q in range(Q):
            pipe_copy(q).wait_recv()

    @pl.when(pipe == sections - 1)
    def _():
        zero_copy().wait()


def copy_kernel(
    out_in, passed_in, fgrad_in, tap_in, out, passed, fgrad, tap, v_out, v_passed, v_fgrad, v_tap, sem
):
    pairs = []
    for n in range(4):
        rows = slice(n * R // 4, (n + 1) * R // 4)
        pairs += [(passed_in.at[w, rows], v_passed.at[w, rows], passed.at[w, rows]) for w in range(3)]
        pairs.append((out_in.at[rows], v_out.at[rows], out.at[rows]))
    pairs += [(fgrad_in, v_fgrad, fgrad), (tap_in, v_tap, tap)]
    into = [pltpu.make_async_copy(a, b, sem.at[0, i]) for i, (a, b, _) in enumerate(pairs)]
    back = [pltpu.make_async_copy(b, c, sem.at[1, i]) for i, (_, b, c) in enumerate(pairs)]
    for copy in into:
        copy.start()
    for first, second in zip(into, back):
        first.wait()
        second.start()
    for copy in back:
        copy.wait()


def local(query_in, key_in, value_in, grad_out, long_filter, short_taps):
    vmem = pl.BlockSpec(memory_space=pltpu.VMEM)
    hbm = pl.BlockSpec(memory_space=pl.ANY)
    dma = pltpu.SemaphoreType.DMA
    layer_out, passed_grads, filter_grad, tap_grads = pl.pallas_call(
        whole_kernel,
        in_specs=[hbm] * 4 + [vmem] * 2,
        out_specs=[hbm, hbm, vmem, vmem],
        out_shape=[
            jax.ShapeDtypeStruct((R, C), bf16),
            jax.ShapeDtypeStruct((3, R, C), bf16),
            jax.ShapeDtypeStruct((R, C // G), f32),
            jax.ShapeDtypeStruct((9, C // TW, TW), f32),
        ],
        scratch_shapes=[
            pltpu.VMEM((4, R, C), bf16),
            pltpu.VMEM((R, C), bf16),
            pltpu.VMEM((3, R, C), f32),
            pltpu.VMEM((Q, N, 2, OC, R), bf16),
            pltpu.VMEM((Q, N, 2, OC, R), bf16),
            pltpu.VMEM((Q, N, 2, OC, R), bf16),
            pltpu.VMEM((Q, N, 2, OC, R), bf16),
            pltpu.VMEM((Q * GQ, R, R + T), bf16),
            pltpu.VMEM((Q * GQ, 8, T), f32),
            pltpu.VMEM((R, T), f32),
            pltpu.VMEM((Q * GQ, 8, T), f32),
            pltpu.VMEM((Q, 3, R, CQ), bf16),
            pltpu.VMEM((3, R, C), bf16),
            pltpu.VMEM((Q, 16, W), f32),
            pltpu.VMEM((Q, 16, W), bf16),
            pltpu.VMEM((Q, 16, W), bf16),
            pltpu.VMEM((16, W), f32),
            pltpu.VMEM((Q, 16, W), bf16),
            pltpu.VMEM((Q, 16, W), bf16),
            pltpu.VMEM((N, Q * GQ, R), f32),
            pltpu.VMEM((N, Q * GQ, R), bf16),
            pltpu.VMEM((N, Q * GQ, R), bf16),
            pltpu.VMEM((N, Q * GQ, R), f32),
            pltpu.VMEM((N, Q * GQ, R), f32),
            pltpu.VMEM((C // G, R), f32),
            pltpu.VMEM((HALVES, N, 9, TW), f32),
            pltpu.VMEM((HALVES, N, 9, TW), f32),
            pltpu.VMEM((HALVES, 9, TW), f32),
            pltpu.VMEM((HALVES, N, 9, TW), f32),
            dma((Q,)), dma((Q,)),
            dma((N,)), dma((N,)),
            dma((Q, N)), dma((Q, N)),
            dma((Q, N)), dma((Q, N)),
            dma((Q,)), dma((Q,)),
            dma((Q,)), dma((Q,)),
            dma((N,)), dma((N,)),
            dma((HALVES, N)), dma((HALVES, N)),
            dma((HALVES, N)), dma((HALVES, N)),
            dma,
            dma((4,)),
            dma((Q,)),
        ],
        compiler_params=pltpu.CompilerParams(
            collective_id=0, has_side_effects=True, vmem_limit_bytes=60 * 2**20
        ),
    )(query_in[0], key_in[0], value_in[0], grad_out[0], long_filter[0],
      short_taps[0].reshape(9, 1, C))
    layer_out, passed_grads, filter_grad, tap_grads = pl.pallas_call(
        copy_kernel,
        in_specs=[hbm] * 4,
        out_specs=[hbm] * 4,
        out_shape=[
            jax.ShapeDtypeStruct((R, C), bf16),
            jax.ShapeDtypeStruct((3, R, C), bf16),
            jax.ShapeDtypeStruct((R, C // G), f32),
            jax.ShapeDtypeStruct((9, C // TW, TW), f32),
        ],
        scratch_shapes=[
            pltpu.VMEM((R, C), bf16),
            pltpu.VMEM((3, R, C), bf16),
            pltpu.VMEM((R, C // G), f32),
            pltpu.VMEM((9, C // TW, TW), f32),
            dma((2, 18)),
        ],
        compiler_params=pltpu.CompilerParams(vmem_limit_bytes=60 * 2**20),
    )(layer_out, passed_grads, filter_grad, tap_grads)
    tap_grads = tap_grads.reshape(1, 3, 3, C)
    return (layer_out[None], passed_grads[None], filter_grad[None], tap_grads)


def solution(mesh):
    in_specs = (
        P("pipe", "seq", None),
        P("pipe", "seq", None),
        P("pipe", "seq", None),
        P("pipe", "seq", None),
        P("pipe", "seq", None),
        P("pipe", None, None, None),
    )
    out_specs = (
        P("pipe", "seq", None),
        P("pipe", None, "seq", None),
        P("pipe", "seq", None),
        P("pipe", None, None, None),
    )
    return jax.shard_map(local, mesh=mesh, in_specs=in_specs, out_specs=out_specs, check_vma=False)
```

```python
import functools
import math

import jax
import jax.numpy as jnp
from jax import lax
from jax.experimental import pallas as pl
from jax.experimental.pallas import tpu as pltpu
from jax.sharding import PartitionSpec as P

f32 = jnp.float32
bf16 = jnp.bfloat16

N = 16
R = 128
C = 4096
Q = 8
CQ = C // Q
G = 16
OC = CQ // N
GQ = OC // G
T = N * R
W = 256
B = CQ // W
HALVES = 2
TW = C // N // HALVES
AHEAD = 2
LAG = 1


def rows_down(x, first):
    row = lax.broadcasted_iota(jnp.int32, x.shape, 0)
    return jnp.where(row == 0, first, pltpu.roll(x, 1, 0))


def rows_up(x, last):
    row = lax.broadcasted_iota(jnp.int32, x.shape, 0)
    return jnp.where(row == x.shape[0] - 1, last, pltpu.roll(x, x.shape[0] - 1, 0))


def short_filter(x, halo2, halo1, taps):
    back1 = rows_down(x, halo1)
    back2 = rows_down(back1, halo2)
    return taps[0] * x + taps[1] * back1 + taps[2] * back2


def features(lanes, in_refs, halo, taps_ref):
    out = []
    for w in range(3):
        x = in_refs[w][:, lanes].astype(f32)
        taps = [taps_ref[3 * w + j, :, lanes] for j in range(3)]
        out.append(short_filter(x, halo[2 * w : 2 * w + 1], halo[2 * w + 1 : 2 * w + 2], taps))
    return out


def eight_rows(ref, b):
    rows = ref[...].astype(f32)
    return jnp.where(b == 0, rows[0:8], rows[8:16])


def build_base(h, base_ref):
    for r in range(8):
        base_ref[:, r, :] = h if r == 0 else pltpu.roll(h, r, 1)


def build_band(base, band_ref):
    band_ref[:, 0:R] = jnp.zeros((R, R), bf16)
    for m in range(R // 16):
        low = base if m == 0 else pltpu.roll(base, 16 * m, 1)
        high = pltpu.roll(base, 16 * m + 8, 1)
        both = jnp.concatenate([low, high], axis=0)
        row = lax.broadcasted_iota(jnp.int32, (16, R), 0) + 16 * m
        lane = lax.broadcasted_iota(jnp.int32, (16, R), 1)
        rows = slice(16 * m, 16 * m + 16)
        band_ref[rows, R : 2 * R] = jnp.where(lane >= row, both[:, :R], 0.0).astype(bf16)
        band_ref[rows, 2 * R :] = both[:, R:].astype(bf16)


def pair_lanes(x):
    v = x.reshape(N // 2, 2, G, R)
    return jnp.concatenate([v[:, 0], v[:, 1]], axis=-1).reshape(N // 2 * G, 2 * R)


def convolve(x, s, band):
    x2, s2 = pair_lanes(x), pair_lanes(s)
    zeros = jnp.zeros(((N // 2 - 1) * G, 2 * R), bf16)
    xp = jnp.concatenate([zeros, x2], axis=0)
    sp = jnp.concatenate([s2, zeros], axis=0)
    rows = N // 2 * G
    conv = back = None
    for d in range(N // 2):
        w = jnp.concatenate(
            [
                band[:, R + 2 * R * d : R + 2 * R * d + 2 * R],
                band[:, 2 * R * d : 2 * R * d + 2 * R],
            ],
            axis=0,
        )
        top = (N // 2 - 1 - d) * G
        c = jnp.dot(xp[top : top + rows], w, preferred_element_type=f32)
        b = lax.dot_general(
            sp[d * G : d * G + rows], w, (((1,), (1,)), ((), ())), preferred_element_type=f32
        )
        conv = c if conv is None else conv + c
        back = b if back is None else back + b
    return conv, back


def correlate(x, s, gram_ref):
    xt = x.reshape(N * G, R).astype(f32).T.astype(bf16)
    sp = jnp.concatenate([s.reshape(N * G, R), jnp.zeros((N * G, R), bf16)], axis=0)
    for d in range(N // 2):
        right = jnp.concatenate(
            [sp[2 * d * G : 2 * d * G + N * G], sp[(2 * d + 1) * G : (2 * d + 1) * G + N * G]],
            axis=1,
        )
        gram = jnp.dot(xt, right, preferred_element_type=f32)
        if d == 0:
            row = lax.broadcasted_iota(jnp.int32, gram.shape, 0)
            lane = lax.broadcasted_iota(jnp.int32, gram.shape, 1)
            gram = jnp.where(lane >= row, gram, 0.0)
        gram_ref[:, 2 * R * d : 2 * R * d + 2 * R] = gram
    total = gram_ref[0:8, :]
    for m in range(1, R // 8):
        total = total + pltpu.roll(gram_ref[8 * m : 8 * m + 8, :], T - 8 * m, 1)
    return total


def block(n, size):
    return pl.ds(pl.multiple_of(n * size, size), size)


def whole_kernel(
    q_hbm, k_hbm, v_hbm, g_hbm, filter_ref, taps_ref,
    out_hbm, passed_ref, fgrad_ref, tap_ref,
    inputs, out_ref, feat, send, recv, ret_send, ret_recv, band, base, gram, fold, slabs, zeros,
    halo_pack, halo_out, halo_in, edge_pack, edge_out, edge_in, filt_pack, filt_out, filt_in, fg_out, fg_in, fg_rows,
    tap_out, tap_in, sum_out, sum_in,
    s_halo, r_halo, s_filt, r_filt, s_fwd, r_fwd, s_ret, r_ret, s_edge, r_edge,
    s_pipe, r_pipe, s_fg, r_fg, s_tap, r_tap, s_sum, r_sum, s_zero, s_in, s_out,
):
    me = lax.axis_index("seq")
    pipe = lax.axis_index("pipe")
    sections = lax.axis_size("pipe")
    raw = tuple(inputs.at[w] for w in range(3))
    g_ref = inputs.at[3]

    def load(w):
        return pltpu.make_async_copy((q_hbm, k_hbm, v_hbm, g_hbm)[w], inputs.at[w], s_in.at[w])

    for w in range(4):
        load(w).start()

    def peer_of(s):
        half = lax.div(s + 1, 2)
        return lax.rem(me + N + half * (2 * lax.rem(s, 2) - 1), N)

    def each_peer(fn):
        def step(s, carry):
            fn(peer_of(s))
            return carry

        lax.fori_loop(1, N, step, 0, unroll=True)

    def remote(src, dst, s_sem, r_sem, where):
        return pltpu.make_async_remote_copy(
            src_ref=src, dst_ref=dst, send_sem=s_sem, recv_sem=r_sem,
            device_id=where, device_id_type=pl.DeviceIdType.MESH,
        )

    def spread(src, dst, s_sem, r_sem):
        def start(k):
            remote(src.at[k], dst.at[me], s_sem.at[k], r_sem.at[me], {"seq": k}).start()

        def wait_recv(k):
            remote(src.at[k], dst.at[k], s_sem.at[k], r_sem.at[k], {"seq": k}).wait_recv()

        def wait_send(k):
            remote(src.at[k], dst.at[k], s_sem.at[k], r_sem.at[k], {"seq": k}).wait_send()

        return start, wait_recv, wait_send

    barrier = pltpu.get_barrier_semaphore()

    def greet(k):
        pl.semaphore_signal(
            barrier, inc=1, device_id={"seq": k}, device_id_type=pl.DeviceIdType.MESH
        )

    each_peer(greet)
    for by in (1, sections - 1):
        pl.semaphore_signal(
            barrier, inc=1, device_id={"pipe": lax.rem(pipe + by, sections)},
            device_id_type=pl.DeviceIdType.MESH,
        )

    for w in range(4):
        load(w).wait()
    halo_pack[...] = jnp.zeros_like(halo_pack)
    for w in range(3):
        last = raw[w][R - 16 : R, :].astype(f32)[14:16]
        for q in range(Q):
            for b in range(B):
                first = q * CQ + b * W
                halo_pack[q, 8 * b + 2 * w : 8 * b + 2 * w + 2, :] = last[:, first : first + W]
    halo_out[...] = halo_pack[...].astype(bf16)

    pl.semaphore_wait(barrier, N + 1)

    def halo_copy(q):
        return remote(
            halo_out.at[q], halo_in.at[q], s_halo.at[q], r_halo.at[q],
            {"seq": jnp.minimum(me + 1, N - 1)},
        )

    @pl.when(me < N - 1)
    def _():
        for q in range(Q):
            halo_copy(q).start()

    turned = filter_ref[...].T
    for k in range(N):
        for q in range(Q):
            first = q * N * GQ + k * GQ
            filt_pack[k, q * GQ : (q + 1) * GQ, :] = turned[first : first + GQ]
    filt_out[...] = filt_pack[...].astype(bf16)
    filt_in[me] = filt_out[me]
    filt = spread(filt_out, filt_in, s_filt, r_filt)
    each_peer(filt[0])

    @pl.when(me == 0)
    def _():
        halo_in[...] = jnp.zeros_like(halo_in)

    def fwd(q):
        return spread(send.at[q], recv.at[q], s_fwd.at[q], r_fwd.at[q])

    def ret(q):
        return spread(ret_send.at[q], ret_recv.at[q], s_ret.at[q], r_ret.at[q])

    def feature_phase(q):
        @pl.when(me > 0)
        def _():
            halo_copy(q).wait_recv()

        def step(b, carry):
            n = q * B + b
            lanes = block(n, W)
            query, keyed, valued = features(lanes, raw, eight_rows(halo_in.at[q], b), taps_ref)
            feat[0, :, lanes] = query
            feat[1, :, lanes] = keyed
            feat[2, :, lanes] = valued
            product = (keyed * valued).astype(bf16).astype(f32).T
            scaled = (g_ref[:, lanes].astype(f32) * query).astype(bf16).astype(f32).T
            for i in range(W // OC):
                send[q, b * (W // OC) + i, 0] = product[i * OC : (i + 1) * OC].astype(bf16)
                send[q, b * (W // OC) + i, 1] = scaled[i * OC : (i + 1) * OC].astype(bf16)
            return carry

        lax.fori_loop(0, B, step, 0)
        each_peer(fwd(q)[0])
        recv[q, me] = send[q, me]

    def band_phase(q):
        def group(i, carry):
            build_band(base[q * GQ + i], band.at[q * GQ + i])
            return carry

        lax.fori_loop(0, GQ, group, 0)

    def conv_phase(q):
        each_peer(fwd(q)[1])

        def group(i, carry):
            rows = block(i, G)
            conv, back = convolve(
                recv[q, :, 0, rows, :], recv[q, :, 1, rows, :], band.at[q * GQ + i]
            )
            for w, value in ((0, conv), (1, back)):
                value = value.astype(bf16)
                for half in range(2):
                    part = value[:, half * R : (half + 1) * R]
                    for j in range(N // 2):
                        ret_send[q, 2 * j + half, w, rows, :] = part[j * G : (j + 1) * G]
            return carry

        lax.fori_loop(0, GQ, group, 0)
        each_peer(ret(q)[0])
        ret_recv[q, me] = ret_send[q, me]

    def corr_phase(q):
        def group(i, carry):
            rows = block(i, G)
            fold[q * GQ + i] = correlate(
                recv[q, :, 0, rows, :], recv[q, :, 1, rows, :], gram
            )
            return carry

        lax.fori_loop(0, GQ, group, 0)

    def edge_copy(q):
        return remote(
            edge_out.at[q], edge_in.at[q], s_edge.at[q], r_edge.at[q],
            {"seq": jnp.maximum(me - 1, 0)},
        )

    def out_copy(q):
        lanes = block(q, CQ)
        return pltpu.make_async_copy(out_ref.at[:, lanes], out_hbm.at[:, lanes], s_out.at[q])

    def grad_phase(q):
        each_peer(ret(q)[1])

        def step(b, carry):
            lanes = block(q * B + b, W)
            owners = W // OC
            got = [
                jnp.concatenate(
                    [ret_recv[q, b * owners + i, w].astype(f32) for i in range(owners)], axis=0
                ).T
                for w in range(2)
            ]
            conv, back = got
            grad = g_ref[:, lanes].astype(f32)
            out_ref[:, lanes] = (feat[0, :, lanes] * conv).astype(bf16)
            grads = (grad * conv, back * feat[2, :, lanes], back * feat[1, :, lanes])
            for w in range(3):
                feat[w, :, lanes] = grads[w]
            rows = [g[0:2] for g in grads] + [jnp.zeros((2, W), f32)]
            edge_pack[block(b, 8), :] = jnp.concatenate(rows, axis=0)
            return carry

        lax.fori_loop(0, B, step, 0)
        edge_out[q] = edge_pack[...].astype(bf16)

        out_copy(q).start()

        @pl.when(me > 0)
        def _():
            edge_copy(q).start()

        @pl.when(me == N - 1)
        def _():
            edge_in[q] = jnp.zeros((16, W), bf16)

    def tap(half):
        return spread(tap_out.at[half], tap_in.at[half], s_tap.at[half], r_tap.at[half])

    def pipe_copy(q):
        return remote(
            slabs.at[q], passed_ref.at[:, :, block(q, CQ)], s_pipe.at[q], r_pipe.at[q],
            {"pipe": jnp.maximum(pipe - 1, 0)},
        )

    def input_phase(q):
        @pl.when(me < N - 1)
        def _():
            edge_copy(q).wait_recv()

        def step(b, carry):
            n = q * B + b
            lanes = block(n, W)
            near = block(b, W)
            edge = eight_rows(edge_in.at[q], b)
            for w in range(3):
                g0 = feat[w, :, lanes]
                g1 = rows_up(g0, edge[2 * w : 2 * w + 1])
                g2 = rows_up(g1, edge[2 * w + 1 : 2 * w + 2])
                x = raw[w][:, lanes].astype(f32)
                total = None
                for j, g in enumerate((g0, g1, g2)):
                    term = taps_ref[3 * w + j, :, lanes] * g
                    total = term if total is None else total + term
                    part = jnp.sum(g * x, axis=0, keepdims=True)
                    for i in range(W // TW):
                        owner = lax.rem(n * (W // TW) + i, N)
                        half = lax.div(n * (W // TW), N)
                        tap_out[half, owner, 3 * w + j : 3 * w + j + 1, :] = part[:, i * TW : (i + 1) * TW]
                slabs[q, w, :, near] = total.astype(bf16)
            return carry

        lax.fori_loop(0, B, step, 0)

        @pl.when(pipe > 0)
        def _():
            pipe_copy(q).start()

        for half in range(HALVES):

            @pl.when(q == (half + 1) * (Q // HALVES) - 1)
            def _():
                each_peer(tap(half)[0])
                tap_in[half, me] = tap_out[half, me]

    def filter_phase():
        each_peer(filt[1])
        h = jnp.concatenate([filt_in[j].astype(f32) for j in range(N)], axis=1)
        build_base(h, base)

    fg_start, fg_wait_recv, fg_wait_send = spread(fg_out, fg_in, s_fg, r_fg)

    def unfold_phase():
        total = fold[:, 0, :]
        for r in range(1, 8):
            total = total + pltpu.roll(fold[:, r, :], T - r, 1)
        total = total * (1.0 / math.sqrt(T * G))
        for k in range(N):
            fg_out[k] = total[:, k * R : (k + 1) * R]
        fg_in[me] = fg_out[me]
        each_peer(fg_start)

    def fgrad_phase():
        each_peer(fg_wait_recv)
        for k in range(N):
            for q in range(Q):
                first = q * N * GQ + k * GQ
                fg_rows[first : first + GQ, :] = fg_in[k, q * GQ : (q + 1) * GQ, :]
        fgrad_ref[...] = fg_rows[...].T

    def zero_copy():
        return pltpu.make_async_copy(zeros, passed_ref, s_zero)

    def sum_copy(half, k, slot):
        return remote(
            sum_out.at[half], sum_in.at[half, slot], s_sum.at[half, k], r_sum.at[half, slot], {"seq": k}
        )

    def sum_phase(half):
        each_peer(tap(half)[1])
        owned = tap_in[half, 0]
        for k in range(1, N):
            owned = owned + tap_in[half, k]
        sum_out[half] = owned * (1.0 / math.sqrt(T))
        sum_in[half, me] = sum_out[half]
        each_peer(lambda k: sum_copy(half, k, me).start())

    for q in range(AHEAD):
        feature_phase(q)
    def zero_phase():
        @pl.when(pipe == sections - 1)
        def _():
            zeros[...] = jnp.zeros_like(zeros)
            zero_copy().start()

    filter_phase()
    band_phase(0)

    def step(t, carry):
        @pl.when(t < Q)
        def _():
            conv_phase(t)

        @pl.when((t >= LAG) & (t < Q + LAG))
        def _():
            grad_phase(t - LAG)

        @pl.when(t + AHEAD < Q)
        def _():
            feature_phase(t + AHEAD)

        @pl.when(t + 1 < Q)
        def _():
            band_phase(t + 1)

        @pl.when(t < Q)
        def _():
            corr_phase(t)

        @pl.when(t == Q - 1)
        def _():
            unfold_phase()

        @pl.when(t == 0)
        def _():
            zero_phase()

        @pl.when(t >= LAG + 1)
        def _():
            input_phase(t - LAG - 1)

        @pl.when(t == Q)
        def _():
            sum_phase(0)

        return carry

    lax.fori_loop(0, Q + LAG + 1, step, 0)

    def sent(q, carry):
        each_peer(fwd(q)[2])
        each_peer(ret(q)[2])
        out_copy(q).wait()
        return carry

    fgrad_phase()
    lax.fori_loop(0, Q // 2, sent, 0)
    sum_phase(1)
    lax.fori_loop(Q // 2, Q, sent, 0)

    @pl.when(me < N - 1)
    def _():
        for q in range(Q):
            halo_copy(q).wait_send()

    each_peer(filt[2])
    each_peer(fg_wait_send)
    for half in range(HALVES):
        each_peer(tap(half)[2])
        each_peer(lambda k: sum_copy(half, k, k).wait_send())

    for half in range(HALVES):
        each_peer(lambda k: sum_copy(half, k, k).wait_recv())
        for r in range(9):
            tap_ref[r, half * N : (half + 1) * N, :] = sum_in[half, :, r, :]

    @pl.when(me > 0)
    def _():
        for q in range(Q):
            edge_copy(q).wait_send()

    @pl.when(pipe > 0)
    def _():
        for q in range(Q):
            pipe_copy(q).wait_send()

    @pl.when(pipe < sections - 1)
    def _():
        for q in range(Q):
            pipe_copy(q).wait_recv()

    @pl.when(pipe == sections - 1)
    def _():
        zero_copy().wait()


def copy_kernel(
    out_in, passed_in, fgrad_in, tap_in, out, passed, fgrad, tap, v_out, v_passed, v_fgrad, v_tap, sem
):
    pairs = []
    for n in range(4):
        rows = slice(n * R // 4, (n + 1) * R // 4)
        pairs += [(passed_in.at[w, rows], v_passed.at[w, rows], passed.at[w, rows]) for w in range(3)]
        pairs.append((out_in.at[rows], v_out.at[rows], out.at[rows]))
    pairs += [(fgrad_in, v_fgrad, fgrad), (tap_in, v_tap, tap)]
    into = [pltpu.make_async_copy(a, b, sem.at[0, i]) for i, (a, b, _) in enumerate(pairs)]
    back = [pltpu.make_async_copy(b, c, sem.at[1, i]) for i, (_, b, c) in enumerate(pairs)]
    for copy in into:
        copy.start()
    for first, second in zip(into, back):
        first.wait()
        second.start()
    for copy in back:
        copy.wait()


def local(query_in, key_in, value_in, grad_out, long_filter, short_taps):
    vmem = pl.BlockSpec(memory_space=pltpu.VMEM)
    hbm = pl.BlockSpec(memory_space=pl.ANY)
    dma = pltpu.SemaphoreType.DMA
    layer_out, passed_grads, filter_grad, tap_grads = pl.pallas_call(
        whole_kernel,
        in_specs=[hbm] * 4 + [vmem] * 2,
        out_specs=[hbm, hbm, vmem, vmem],
        out_shape=[
            jax.ShapeDtypeStruct((R, C), bf16),
            jax.ShapeDtypeStruct((3, R, C), bf16),
            jax.ShapeDtypeStruct((R, C // G), f32),
            jax.ShapeDtypeStruct((9, C // TW, TW), f32),
        ],
        scratch_shapes=[
            pltpu.VMEM((4, R, C), bf16),
            pltpu.VMEM((R, C), bf16),
            pltpu.VMEM((3, R, C), f32),
            pltpu.VMEM((Q, N, 2, OC, R), bf16),
            pltpu.VMEM((Q, N, 2, OC, R), bf16),
            pltpu.VMEM((Q, N, 2, OC, R), bf16),
            pltpu.VMEM((Q, N, 2, OC, R), bf16),
            pltpu.VMEM((Q * GQ, R, R + T), bf16),
            pltpu.VMEM((Q * GQ, 8, T), f32),
            pltpu.VMEM((R, T), f32),
            pltpu.VMEM((Q * GQ, 8, T), f32),
            pltpu.VMEM((Q, 3, R, CQ), bf16),
            pltpu.VMEM((3, R, C), bf16),
            pltpu.VMEM((Q, 16, W), f32),
            pltpu.VMEM((Q, 16, W), bf16),
            pltpu.VMEM((Q, 16, W), bf16),
            pltpu.VMEM((16, W), f32),
            pltpu.VMEM((Q, 16, W), bf16),
            pltpu.VMEM((Q, 16, W), bf16),
            pltpu.VMEM((N, Q * GQ, R), f32),
            pltpu.VMEM((N, Q * GQ, R), bf16),
            pltpu.VMEM((N, Q * GQ, R), bf16),
            pltpu.VMEM((N, Q * GQ, R), f32),
            pltpu.VMEM((N, Q * GQ, R), f32),
            pltpu.VMEM((C // G, R), f32),
            pltpu.VMEM((HALVES, N, 9, TW), f32),
            pltpu.VMEM((HALVES, N, 9, TW), f32),
            pltpu.VMEM((HALVES, 9, TW), f32),
            pltpu.VMEM((HALVES, N, 9, TW), f32),
            dma((Q,)), dma((Q,)),
            dma((N,)), dma((N,)),
            dma((Q, N)), dma((Q, N)),
            dma((Q, N)), dma((Q, N)),
            dma((Q,)), dma((Q,)),
            dma((Q,)), dma((Q,)),
            dma((N,)), dma((N,)),
            dma((HALVES, N)), dma((HALVES, N)),
            dma((HALVES, N)), dma((HALVES, N)),
            dma,
            dma((4,)),
            dma((Q,)),
        ],
        compiler_params=pltpu.CompilerParams(
            collective_id=0, has_side_effects=True, vmem_limit_bytes=60 * 2**20
        ),
    )(query_in[0], key_in[0], value_in[0], grad_out[0], long_filter[0],
      short_taps[0].reshape(9, 1, C))
    layer_out, passed_grads, filter_grad, tap_grads = pl.pallas_call(
        copy_kernel,
        in_specs=[hbm] * 4,
        out_specs=[hbm] * 4,
        out_shape=[
            jax.ShapeDtypeStruct((R, C), bf16),
            jax.ShapeDtypeStruct((3, R, C), bf16),
            jax.ShapeDtypeStruct((R, C // G), f32),
            jax.ShapeDtypeStruct((9, C // TW, TW), f32),
        ],
        scratch_shapes=[
            pltpu.VMEM((R, C), bf16),
            pltpu.VMEM((3, R, C), bf16),
            pltpu.VMEM((R, C // G), f32),
            pltpu.VMEM((9, C // TW, TW), f32),
            dma((2, 18)),
        ],
        compiler_params=pltpu.CompilerParams(vmem_limit_bytes=60 * 2**20),
    )(layer_out, passed_grads, filter_grad, tap_grads)
    tap_grads = tap_grads.reshape(1, 3, 3, C)
    return (layer_out[None], passed_grads[None], filter_grad[None], tap_grads)


def solution(mesh):
    in_specs = (
        P("pipe", "seq", None),
        P("pipe", "seq", None),
        P("pipe", "seq", None),
        P("pipe", "seq", None),
        P("pipe", "seq", None),
        P("pipe", None, None, None),
    )
    out_specs = (
        P("pipe", "seq", None),
        P("pipe", None, "seq", None),
        P("pipe", "seq", None),
        P("pipe", None, None, None),
    )
    return jax.shard_map(local, mesh=mesh, in_specs=in_specs, out_specs=out_specs, check_vma=False)
```
